32 devices in a mesh: blk: 16 (over z, y, x), slab: 2 (over core).
Axes of the slice: x: 2, y: 2, z: 4, core: 2. Of those that a mesh axis runs over, the one named last changes fastest.
Arguments:
- amplitudes: bfloat16 [960, 8192], P('blk', 'slab'), may hold values from -6 to 6
- ladder_ints: bfloat16 [8192, 8192], P('slab', 'blk'), may hold values from -0.0625 to 0.0625
- cycle_ints: bfloat16 [2, 64, 120, 512], P('slab', 'blk'), may hold values from -0.0625 to 0.0625
- block_dims: int32 [2, 2], replicated, may hold values from 24 to 64, as said below
Outputs:
- ladder_res: bfloat16 [960, 8192], P('slab', 'blk')
- cycle_res: bfloat16 [2, 512, 512], P('slab', 'blk')
The draws below stay inside these ranges and needn't reach their ends.
Inputs may be any that keep to these rules, and one draw needn't show every extreme that they name: `block_dims`: every block's two sizes lie within the padded size; in every draw some block's first size equals 64 and some block's second size equals 24.
All inputs are finite; a program needn't handle non-finite values.
Results may differ from the reference program's by a relative error of at most 0.0014.
Values may be sent and summed in bfloat16 or wider, within the bound.
No kernel may reach another device: no remote copies, remote signals or barrier semaphores. Data moves between devices by JAX's collectives and lax.ppermute only.
A program may use at most 128 MiB of HBM per device.

```python
import jax
import jax.numpy as jnp
from jax import lax

NO = 120
BS = 64
JW = 8
IW = 8
NSB = 2
IJ = 960


def draw_block_dims(key, part):
    values = jax.random.randint(key, (NSB, 2), BS * 3 // 8, BS + 1)
    row_index = jnp.arange(NSB, dtype=jnp.int32)[:, None]
    column_index = jnp.arange(2, dtype=jnp.int32)[None, :]
    values = jnp.where((row_index == 0) & (column_index == 0), BS, values)
    values = jnp.where((row_index == NSB - 1) & (column_index == 1), BS * 3 // 8, values)
    return values.astype(jnp.int32)


def block_levels(own_key, shape, shards, least, largest):
    loudness = 1.0
    for dim, parts in shards:
        steps = jax.random.uniform(jax.random.fold_in(jax.random.fold_in(own_key, 6), dim), (parts,), jnp.float32, least / len(shards), largest / len(shards))
        loudness = loudness * jnp.repeat(jnp.exp(steps), shape[dim] // parts).reshape((-1,) + (1,) * (len(shape) - 1 - dim))
    return loudness


def scatter_about(rng, extent, scale, most, pieces=(), kind=jnp.bfloat16):
    values = scale * jax.random.normal(rng, extent, jnp.float32)
    if pieces:
        values = values * block_levels(rng, extent, pieces, -0.22, 0.18)
    return jnp.clip(values, -most, most).astype(kind)


def setup_inputs(seed: int = 0) -> dict:
    keys = jax.random.split(jax.random.key(seed), 5)
    amplitudes = scatter_about(keys[0], (IJ, NSB * BS * BS), 1.0, 6.0, ((0, 16), (1, 2)))
    ladder_ints = scatter_about(keys[1], (NSB * BS * BS, NSB * BS * BS), (NSB * BS * BS) ** -0.5, 0.0625, ((0, 2), (1, 16)))
    cycle_ints = scatter_about(keys[2], (NSB, BS, NO, IW * BS), (NO * BS) ** -0.5, 0.0625, ((0, 2), (1, 16)))
    block_dims = draw_block_dims(jax.random.fold_in(keys[4], 71), 0)
    return {"amplitudes": amplitudes, "ladder_ints": ladder_ints, "cycle_ints": cycle_ints, "block_dims": block_dims}


def column_valid(block_dims):
    column = jnp.arange(NSB * BS * BS, dtype=jnp.int32)
    owner = column // (BS * BS)
    first_index = (column // BS) % BS
    second_index = column % BS
    return (first_index < block_dims[owner, 0]) & (second_index < block_dims[owner, 1])


def reference(amplitudes, ladder_ints, cycle_ints, block_dims):
    valid = column_valid(block_dims)
    masked = jnp.where(valid[None, :], amplitudes, jnp.zeros((), amplitudes.dtype))
    left_side = masked.astype(jnp.float32)
    block_width = BS * BS

    def column_block(block_index):
        piece_ints = lax.dynamic_slice_in_dim(ladder_ints, (block_index * block_width).astype(jnp.int32), block_width, 1).astype(jnp.float32)
        return jnp.dot(left_side, piece_ints, precision=lax.Precision.HIGHEST)

    blocks_out = lax.map(column_block, jnp.arange(NSB, dtype=jnp.int32))
    ladder = jnp.transpose(blocks_out, (1, 0, 2)).reshape(IJ, NSB * block_width)
    ladder_res = jnp.where(valid[None, :], ladder, jnp.zeros((), ladder.dtype)).astype(jnp.bfloat16)
    row_virtual = jnp.arange(IW * BS, dtype=jnp.int32) % BS
    column_virtual = jnp.arange(JW * BS, dtype=jnp.int32) % BS
    results = []
    for sector_block in range(NSB):
        amp_block = masked[:, sector_block * block_width:(sector_block + 1) * block_width]
        amp_block = amp_block.reshape(NO, JW, BS, BS).astype(jnp.float32)
        cycle_term = jnp.einsum("cke,kjcd->ejd", cycle_ints[sector_block].astype(jnp.float32), amp_block, precision=lax.Precision.HIGHEST)
        cycle_term = cycle_term.reshape(IW * BS, JW * BS)
        allowed = (row_virtual[:, None] < block_dims[sector_block, 0]) & (column_virtual[None, :] < block_dims[sector_block, 1])
        results.append(jnp.where(allowed, cycle_term, jnp.zeros((), cycle_term.dtype)).astype(jnp.bfloat16))
    cycle_res = jnp.stack(results, 0)
    return (ladder_res, cycle_res)
```

```python
import functools

import jax
import jax.numpy as jnp
import numpy as np
from jax import lax
from jax.experimental import pallas as pl
from jax.experimental.pallas import tpu as pltpu
from jax.sharding import PartitionSpec as P

BS = 64
LEAST = 24
GROUP = 16
PIECE = 64
AXES = ("blk", "slab")


def block_sizes(block_dims, owner):
    blocks_count = block_dims.shape[0]
    select = owner[:, None] == lax.iota(jnp.int32, blocks_count)[None, :]
    size_first = jnp.sum(jnp.where(select, block_dims[None, :, 0], 0), 1)
    size_second = jnp.sum(jnp.where(select, block_dims[None, :, 1], 0), 1)
    return (size_first, size_second)


def column_valid(block_dims, first_column, column_count):
    column = first_column + lax.iota(jnp.int32, column_count)
    owner = column // (BS * BS)
    size_first, size_second = block_sizes(block_dims, owner)
    return (column // BS % BS < size_first) & (column % BS < size_second)


def cycle_allowed(block_dims, slab_index, blk_index, local_rows, columns):
    own_block = jnp.full((1,), slab_index, jnp.int32)
    size_first, size_second = block_sizes(block_dims, own_block)
    row_virtual = (blk_index * local_rows + lax.iota(jnp.int32, local_rows)) % BS
    column_virtual = lax.iota(jnp.int32, columns) % BS
    return (row_virtual[:, None] < size_first[0]) & (column_virtual[None, :] < size_second[0])


def plain(amplitudes, ladder_ints, cycle_ints, block_dims):
    slab_index = lax.axis_index("slab")
    blk_index = lax.axis_index("blk")
    block_width = amplitudes.shape[1]
    valid = column_valid(block_dims, slab_index * block_width, block_width)
    masked = jnp.where(valid[None, :], amplitudes, jnp.zeros((), amplitudes.dtype))
    gathered = lax.all_gather(masked, "blk", axis=0, tiled=True)
    pair_rows = gathered.shape[0]
    ladder_sum = lax.psum_scatter(
        jnp.dot(gathered, ladder_ints, preferred_element_type=jnp.float32),
        "slab",
        scatter_dimension=0,
        tiled=True,
    )
    out_columns = ladder_ints.shape[1]
    out_valid = column_valid(block_dims, blk_index * out_columns, out_columns)
    ladder_res = jnp.where(out_valid[None, :], ladder_sum, 0.0).astype(jnp.bfloat16)
    occupied = cycle_ints.shape[2]
    j_window = pair_rows // occupied
    columns = lax.all_to_all(masked, "blk", split_axis=1, concat_axis=0, tiled=True)
    c_part = cycle_ints.shape[1]
    amp_part = columns.reshape(occupied, j_window, c_part, BS)
    cycle_term = jnp.einsum(
        "cke,kjcd->ejd", cycle_ints[0], amp_part, preferred_element_type=jnp.float32
    )
    cycle_term = cycle_term.reshape(cycle_term.shape[0], j_window * BS)
    cycle_sum = lax.psum_scatter(cycle_term, "blk", scatter_dimension=0, tiled=True)
    allowed = cycle_allowed(block_dims, slab_index, blk_index, cycle_sum.shape[0], j_window * BS)
    cycle_res = jnp.where(allowed, cycle_sum, 0.0).astype(jnp.bfloat16)[None]
    return (ladder_res, cycle_res)


def send(value, target, cores=(0, 1)):
    pairs = []
    for chip in range(16):
        for core in cores:
            x, y, z = target(chip & 1, chip >> 1 & 1, chip >> 2, core)
            pairs.append((2 * chip + core, 2 * (4 * (z % 4) + 2 * y + x) + core))
    return lax.ppermute(value, AXES, pairs)


def along_x(x, y, z, core):
    return (1 - x, y, z)


def along_y(x, y, z, core):
    return (x, 1 - y, z)


def across(x, y, z, core):
    return (1 - x, 1 - y, z)


def first_axis(x, y, z, core):
    return along_x(x, y, z, core) if core == 0 else along_y(x, y, z, core)


def second_axis(x, y, z, core):
    return along_y(x, y, z, core) if core == 0 else along_x(x, y, z, core)


def up(step):
    return lambda x, y, z, core: (x, y, z + step)


def to_other_core(value, cores):
    return lax.ppermute(value, "slab", [(core, 1 - core) for core in cores])


def compact_tables(width):
    column = np.arange(GROUP * width)
    c, d = column // width, column % width
    return np.stack([c * BS + d, c, d] + [c * 0] * 5).astype(np.int32)


def prep_kernel(width, dims, place, amp, moved, wide, narrow, out, rows):
    def tiles(table, group_width):
        result = []
        for lo in range(0, GROUP * group_width, 128):
            start = lo // group_width // 2 * 128
            stop = -(-((lo + 127) // group_width + 1) // 2) * 128
            source = table[0:1, lo : lo + 128] - start
            at = lax.broadcasted_iota(jnp.int32, (stop - start, 128), 0)
            pick = jnp.where(at == source, 1.0, 0.0).astype(jnp.bfloat16)
            result.append((lo, start, stop, pick))
        return result

    def compact(source, base, table, picks, block, first, to):
        for lo, start, stop, pick in picks:
            value = jnp.dot(
                source[:, base + start : base + stop], pick, preferred_element_type=jnp.float32
            )
            c, d = table[1:2, lo : lo + 128] + first, table[2:3, lo : lo + 128]
            keep = (c < dims[block, 0]) & (d < dims[block, 1])
            rows[0:60, to + lo : to + lo + 128] = jnp.where(keep, value, 0.0).astype(jnp.bfloat16)

    group = GROUP * BS
    wide_columns, narrow_columns = GROUP * width, GROUP * LEAST
    rows[...] = jnp.zeros_like(rows)

    @pl.when(place[0] == 0)
    def _():
        picks = tiles(wide, width)
        for g in range(3):
            compact(amp, g * group, wide, picks, 0, g * GROUP, g * wide_columns)

    @pl.when(place[0] == 1)
    def _():
        compact(moved, 0, wide, tiles(wide, width), 0, 3 * GROUP, 0)
        picks = tiles(narrow, LEAST)
        for g in range(4):
            compact(amp, g * group, narrow, picks, 1, g * GROUP, wide_columns + g * narrow_columns)

    shape = (PIECE, PIECE)
    shift = lax.broadcasted_iota(jnp.int32, shape, 0) - lax.broadcasted_iota(jnp.int32, shape, 1)
    shift = jnp.where(shift == place[1], 1.0, 0.0).astype(jnp.bfloat16)
    out[...] = jnp.dot(shift, rows[...], preferred_element_type=jnp.float32).astype(jnp.bfloat16)


def prep(width, columns, block_dims, place, amplitudes, moved):
    smem = pl.BlockSpec(memory_space=pltpu.SMEM)
    vmem = pl.BlockSpec(memory_space=pltpu.VMEM)
    return pl.pallas_call(
        functools.partial(prep_kernel, width),
        out_shape=jax.ShapeDtypeStruct((PIECE, columns), jnp.bfloat16),
        in_specs=[smem, smem] + [vmem] * 4,
        out_specs=vmem,
        scratch_shapes=[pltpu.VMEM((PIECE, columns), jnp.bfloat16)],
        name="prep",
    )(
        block_dims,
        place,
        amplitudes,
        moved,
        jnp.asarray(compact_tables(width)),
        jnp.asarray(compact_tables(LEAST)),
    )


def compact_rows(ladder_ints, moved_ints, width, columns, core):
    def pad(rows):
        return jnp.pad(rows, ((0, columns - rows.shape[0]), (0, 0)))

    def cut(rows, keep):
        out_columns = rows.shape[1]
        return rows.reshape(-1, BS, out_columns)[:, :keep].reshape(-1, out_columns)

    def of_first():
        return pad(cut(ladder_ints[: 3 * GROUP * BS], width))

    def of_second():
        return pad(jnp.concatenate([cut(moved_ints, width), cut(ladder_ints, LEAST)]))

    return lax.cond(core == 0, of_first, of_second)


def slot_of(distance, core):
    swapped = (distance & 1) * 2 + (distance >> 1)
    return jnp.where(core == 0, distance, swapped)


def share_cycle_ints(cycle_ints, blk_index):
    plane = blk_index % 4
    c_part, occupied, rows = cycle_ints.shape[1:]
    column = lax.iota(jnp.int32, rows)
    source = column % 128 // 32 * 128 + (plane ^ (column // 128)) * 32 + column % 32
    pick = (lax.iota(jnp.int32, rows)[:, None] == source[None, :]).astype(jnp.bfloat16)
    turned = jnp.dot(
        cycle_ints.reshape(c_part * occupied, rows), pick, preferred_element_type=jnp.float32
    ).astype(jnp.bfloat16)
    parts = [turned[:, 128 * n : 128 * n + 128] for n in range(4)]
    parts = [
        parts[0],
        send(parts[1], along_x),
        send(parts[2], along_y),
        send(parts[3], across),
    ]
    parts = jnp.stack(parts).reshape(4, c_part, occupied, 128)
    return jnp.concatenate([lax.dynamic_index_in_dim(parts, plane ^ n, 0, False) for n in range(4)])


def slots_of_pieces(shared, order):
    c_count, occupied, rows = shared.shape
    pairs = shared.reshape(c_count, 8, 15, rows)
    slots = jnp.concatenate([pairs[:, :, None, 0:8], pairs[:, :, None, 7:15]], 2)
    slots = slots.reshape(c_count, 16, 8, rows)
    return jnp.concatenate(
        [lax.dynamic_slice_in_dim(slots, chip, 1, 1) for chip in order], 1
    ).reshape(c_count * 128, rows)


def compacted(width, amplitudes, ladder_ints, cycle_ints, block_dims, moved, moved_ints):
    core = lax.axis_index("slab")
    blk_index = lax.axis_index("blk")
    plane, z = blk_index % 4, blk_index // 4
    wide_columns, narrow_columns = GROUP * width, GROUP * LEAST
    columns = max(3 * wide_columns, wide_columns + 4 * narrow_columns)
    early = int(round(0.22 * columns / 128)) * 128

    place = jnp.stack([core, blk_index % 2 * 4]).astype(jnp.int32)
    own = prep(width, columns, block_dims, place, amplitudes, moved)
    line = [send(own[:, early:], up(step)) for step in (1, 2, 3)]
    plane_1 = send(own, first_axis)
    plane_2 = send(own, second_axis)
    plane_12 = send(plane_1, second_axis)
    shared = share_cycle_ints(cycle_ints, blk_index)
    rows_w = compact_rows(ladder_ints, moved_ints, width, columns, core)
    of_plane = jnp.stack([own, plane_1, plane_2, plane_12])
    plane_early = of_plane[:, :, :early]
    early_line = [send(plane_early, up(step)) for step in (1, 2, 3)]
    line = jnp.stack(line)
    line_1 = send(line, first_axis)
    line_2 = send(line, second_axis)
    line_12 = send(line_1, second_axis)

    late = jnp.stack([line, line_1, line_2, line_12], 1)
    early_rest = jnp.stack(early_line)
    pieces = jnp.concatenate(
        [of_plane[None], jnp.concatenate([early_rest, late], 3)]
    ).reshape(16, PIECE, columns)

    out_columns = ladder_ints.shape[1]
    sums = jnp.dot(
        pieces.reshape(16 * PIECE, columns), rows_w, preferred_element_type=jnp.float32
    ).reshape(16, PIECE, out_columns)

    def lies(chip):
        return (z - chip // 4) % 4 * 4 + slot_of(plane ^ (chip % 4), core)

    def half(which):
        return jnp.concatenate(
            [lax.dynamic_slice_in_dim(sums, lies(8 * which + n), 1, 0) for n in range(8)]
        )

    total = half(core) + to_other_core(half(1 - core), (0, 1))
    total = total.reshape(4, 2, PIECE, out_columns)
    total = jnp.concatenate([total[:, 0, :60], total[:, 1, 4:]], 1).reshape(480, out_columns)
    out_valid = column_valid(block_dims, blk_index * out_columns, out_columns)
    ladder_res = jnp.where(out_valid[None, :], total, 0.0).astype(jnp.bfloat16)

    order = [
        (z - n // 4) % 4 * 4 + (plane ^ slot_of(jnp.int32(n % 4), core)) for n in range(16)
    ]
    slots = slots_of_pieces(shared, order)
    rows_here = pieces.reshape(16 * PIECE, columns)
    third = to_other_core(rows_here[:, :wide_columns], (1,)).reshape(4, 4, PIECE, wide_columns)
    third = jnp.stack([third[:, n] for n in (0, 2, 1, 3)], 1).reshape(16 * PIECE, wide_columns)

    def cycle_part(part, group_width):
        part = part.reshape(128, 8, GROUP, group_width).transpose(2, 0, 1, 3)
        part = part.reshape(GROUP * 128, 8 * group_width)
        term = lax.dot_general(
            slots, part, (((0,), (0,)), ((), ())), preferred_element_type=jnp.float32
        )
        term = term.reshape(128, 8, group_width)
        return jnp.pad(term, ((0, 0), (0, 0), (0, BS - group_width))).reshape(4, 32, 8 * BS)

    def of_first():
        mine = lax.dynamic_slice_in_dim(
            rows_here, jnp.minimum(z, 2) * wide_columns, wide_columns, 1
        )
        return cycle_part(jnp.where(z == 3, third, mine), width)

    def of_second():
        mine = lax.dynamic_slice_in_dim(
            rows_here, wide_columns + z * narrow_columns, narrow_columns, 1
        )
        return cycle_part(mine, LEAST)

    term = lax.cond(core == 0, of_first, of_second)

    def chunk(chip_z):
        return lax.dynamic_index_in_dim(term, chip_z % 4, 0, False)

    cycle_sum = chunk(z)
    for step in (1, 2, 3):
        cycle_sum = cycle_sum + send(chunk(z + step), up(step))
    allowed = cycle_allowed(block_dims, core, blk_index, 32, 8 * BS)
    cycle_res = jnp.where(allowed, cycle_sum, 0.0).astype(jnp.bfloat16)[None]
    return (ladder_res, cycle_res)


WIDTHS = (24, 32, 40, 48, 56, 64)


def local(amplitudes, ladder_ints, cycle_ints, block_dims):
    moved = to_other_core(amplitudes[:, 3 * GROUP * BS :], (0,))
    moved_ints = to_other_core(ladder_ints[3 * GROUP * BS :], (0,))
    choice = jnp.maximum(block_dims[0, 1] - LEAST + 7, 0) // 8
    choice = jnp.where(block_dims[1, 1] <= LEAST, choice, len(WIDTHS))
    branches = [functools.partial(compacted, width) for width in WIDTHS]
    branches.append(lambda a, l, c, d, m, n: plain(a, l, c, d))
    return lax.switch(
        choice, branches, amplitudes, ladder_ints, cycle_ints, block_dims, moved, moved_ints
    )


def solution(mesh):
    in_specs = (P("blk", "slab"), P("slab", "blk"), P("slab", "blk", None, None), P())
    out_specs = (P("slab", "blk"), P("slab", "blk", None))
    body = local if dict(mesh.shape) == {"blk": 16, "slab": 2} else plain
    return jax.shard_map(body, mesh=mesh, in_specs=in_specs, out_specs=out_specs, check_vma=False)
```

```python
import functools

import jax
import jax.numpy as jnp
import numpy as np
from jax import lax
from jax.experimental import pallas as pl
from jax.experimental.pallas import tpu as pltpu
from jax.sharding import PartitionSpec as P

BS = 64
LEAST = 24
GROUP = 16
PIECE = 64
AXES = ("blk", "slab")


def block_sizes(block_dims, owner):
    blocks_count = block_dims.shape[0]
    select = owner[:, None] == lax.iota(jnp.int32, blocks_count)[None, :]
    size_first = jnp.sum(jnp.where(select, block_dims[None, :, 0], 0), 1)
    size_second = jnp.sum(jnp.where(select, block_dims[None, :, 1], 0), 1)
    return (size_first, size_second)


def column_valid(block_dims, first_column, column_count):
    column = first_column + lax.iota(jnp.int32, column_count)
    owner = column // (BS * BS)
    size_first, size_second = block_sizes(block_dims, owner)
    return (column // BS % BS < size_first) & (column % BS < size_second)


def cycle_allowed(block_dims, slab_index, blk_index, local_rows, columns):
    own_block = jnp.full((1,), slab_index, jnp.int32)
    size_first, size_second = block_sizes(block_dims, own_block)
    row_virtual = (blk_index * local_rows + lax.iota(jnp.int32, local_rows)) % BS
    column_virtual = lax.iota(jnp.int32, columns) % BS
    return (row_virtual[:, None] < size_first[0]) & (column_virtual[None, :] < size_second[0])


def plain(amplitudes, ladder_ints, cycle_ints, block_dims):
    slab_index = lax.axis_index("slab")
    blk_index = lax.axis_index("blk")
    block_width = amplitudes.shape[1]
    valid = column_valid(block_dims, slab_index * block_width, block_width)
    masked = jnp.where(valid[None, :], amplitudes, jnp.zeros((), amplitudes.dtype))
    gathered = lax.all_gather(masked, "blk", axis=0, tiled=True)
    pair_rows = gathered.shape[0]
    ladder_sum = lax.psum_scatter(
        jnp.dot(gathered, ladder_ints, preferred_element_type=jnp.float32),
        "slab",
        scatter_dimension=0,
        tiled=True,
    )
    out_columns = ladder_ints.shape[1]
    out_valid = column_valid(block_dims, blk_index * out_columns, out_columns)
    ladder_res = jnp.where(out_valid[None, :], ladder_sum, 0.0).astype(jnp.bfloat16)
    occupied = cycle_ints.shape[2]
    j_window = pair_rows // occupied
    columns = lax.all_to_all(masked, "blk", split_axis=1, concat_axis=0, tiled=True)
    c_part = cycle_ints.shape[1]
    amp_part = columns.reshape(occupied, j_window, c_part, BS)
    cycle_term = jnp.einsum(
        "cke,kjcd->ejd", cycle_ints[0], amp_part, preferred_element_type=jnp.float32
    )
    cycle_term = cycle_term.reshape(cycle_term.shape[0], j_window * BS)
    cycle_sum = lax.psum_scatter(cycle_term, "blk", scatter_dimension=0, tiled=True)
    allowed = cycle_allowed(block_dims, slab_index, blk_index, cycle_sum.shape[0], j_window * BS)
    cycle_res = jnp.where(allowed, cycle_sum, 0.0).astype(jnp.bfloat16)[None]
    return (ladder_res, cycle_res)


def send(value, target, cores=(0, 1)):
    pairs = []
    for chip in range(16):
        for core in cores:
            x, y, z = target(chip & 1, chip >> 1 & 1, chip >> 2, core)
            pairs.append((2 * chip + core, 2 * (4 * (z % 4) + 2 * y + x) + core))
    return lax.ppermute(value, AXES, pairs)


def along_x(x, y, z, core):
    return (1 - x, y, z)


def along_y(x, y, z, core):
    return (x, 1 - y, z)


def across(x, y, z, core):
    return (1 - x, 1 - y, z)


def first_axis(x, y, z, core):
    return along_x(x, y, z, core) if core == 0 else along_y(x, y, z, core)


def second_axis(x, y, z, core):
    return along_y(x, y, z, core) if core == 0 else along_x(x, y, z, core)


def up(step):
    return lambda x, y, z, core: (x, y, z + step)


def to_other_core(value, cores):
    return lax.ppermute(value, "slab", [(core, 1 - core) for core in cores])


def compact_tables(width):
    column = np.arange(GROUP * width)
    c, d = column // width, column % width
    return np.stack([c * BS + d, c // 4 * GROUP + c % 4, d] + [c * 0] * 5).astype(np.int32)


def prep_kernel(width, least, dims, amp, moved, wide, narrow, out, rows):
    def tiles(table, group_width):
        result = []
        for lo in range(0, GROUP * group_width, 128):
            start = lo // group_width // 2 * 128
            stop = -(-((lo + 127) // group_width + 1) // 2) * 128
            source = table[0:1, lo : lo + 128] - start
            at = lax.broadcasted_iota(jnp.int32, (stop - start, 128), 0)
            pick = jnp.where(at == source, 1.0, 0.0).astype(jnp.bfloat16)
            result.append((lo, start, stop, pick))
        return result

    def compact(source, group, table, picks, block, to):
        def part(at):
            column = at // (4 * BS) * (GROUP * BS) + group * (4 * BS) + at % (4 * BS)
            return source[:, column : column + 128]

        for lo, start, stop, pick in picks:
            window = jnp.concatenate([part(at) for at in range(start, stop, 128)], 1)
            value = jnp.dot(window, pick, preferred_element_type=jnp.float32)
            c, d = table[1:2, lo : lo + 128] + 4 * group, table[2:3, lo : lo + 128]
            keep = (c < dims[block, 0]) & (d < dims[block, 1])
            rows[0:60, to + lo : to + lo + 128] = jnp.where(keep, value, 0.0).astype(jnp.bfloat16)

    core, shift = lax.axis_index("slab"), lax.axis_index("blk") % 2 * 4
    wide_columns, narrow_columns = GROUP * width, GROUP * least
    rows[...] = jnp.zeros_like(rows)

    @pl.when(core == 0)
    def _():
        picks = tiles(wide, width)
        for g in range(3):
            compact(amp, g, wide, picks, 0, g * wide_columns)

    @pl.when(core == 1)
    def _():
        compact(moved, 3, wide, tiles(wide, width), 0, 0)
        picks = tiles(narrow, least)
        for g in range(4):
            compact(amp, g, narrow, picks, 1, wide_columns + g * narrow_columns)

    shape = (PIECE, PIECE)
    down = lax.broadcasted_iota(jnp.int32, shape, 0) - lax.broadcasted_iota(jnp.int32, shape, 1)
    down = jnp.where(down == shift, 1.0, 0.0).astype(jnp.bfloat16)
    out[...] = jnp.dot(down, rows[...], preferred_element_type=jnp.float32).astype(jnp.bfloat16)


def prep(width, least, columns, block_dims, amplitudes, moved):
    smem = pl.BlockSpec(memory_space=pltpu.SMEM)
    vmem = pl.BlockSpec(memory_space=pltpu.VMEM)
    return pl.pallas_call(
        functools.partial(prep_kernel, width, least),
        out_shape=jax.ShapeDtypeStruct((PIECE, columns), jnp.bfloat16),
        in_specs=[smem] + [vmem] * 4,
        out_specs=vmem,
        scratch_shapes=[pltpu.VMEM((PIECE, columns), jnp.bfloat16)],
        name="prep",
    )(
        block_dims,
        amplitudes,
        moved,
        jnp.asarray(compact_tables(width)),
        jnp.asarray(compact_tables(least)),
    )


def compact_rows(ladder_ints, moved_ints, width, least, columns, core):
    def pad(rows):
        return jnp.pad(rows, ((0, columns - rows.shape[0]), (0, 0)))

    out_columns = ladder_ints.shape[1]

    def cut(rows, keep):
        rows = rows.reshape(4, -1, 4, BS, out_columns)[:, :, :, :keep]
        return rows.transpose(1, 0, 2, 3, 4).reshape(-1, out_columns)

    def of_first():
        groups = ladder_ints.reshape(4, 4, 4 * BS, out_columns)
        return pad(cut(groups[:, :3], width))

    def of_second():
        return pad(jnp.concatenate([cut(moved_ints, width), cut(ladder_ints, least)]))

    return lax.cond(core == 0, of_first, of_second)


def distance_of(slot, core):
    swapped = (slot & 1) * 2 + (slot >> 1)
    return jnp.where(core == 0, slot, swapped)


def chip_of(n, core, blk_index):
    near = (n >= 4) & (n < 12)
    z_step = jnp.where(near, (n & 1) * 2 + 1, jnp.where(n < 4, 0, 2))
    slot = jnp.where(near, (n - 4) >> 1, n & 3)
    z = (blk_index // 4 - z_step) & 3
    return z * 4 + ((blk_index & 3) ^ distance_of(slot, core))


VMEM = pl.BlockSpec(memory_space=pltpu.VMEM)
SMEM = pl.BlockSpec(memory_space=pltpu.SMEM)
ROOM = pltpu.CompilerParams(vmem_limit_bytes=48 * 1024 * 1024)
EARLY_PIECES = 10


def slots_kernel(part_0, part_1, part_2, part_3, early, late, other_early, other_late):
    core, blk_index = lax.axis_index("slab"), lax.axis_index("blk")
    occupied = part_0.shape[1]
    slot = lax.broadcasted_iota(jnp.int32, (128, 1), 0)
    at = lax.broadcasted_iota(jnp.int32, (128, occupied), 1)
    cut = 8 * EARLY_PIECES
    rest = 128 - cut
    for order, first_pieces, last_pieces in ((core, early, late), (1 - core, other_early, other_late)):
        chip = chip_of(slot >> 3, order, blk_index)
        k = 15 * (chip >> 1) + 7 * (chip & 1) + (slot & 7)
        pick = jnp.where(at == k, 1.0, 0.0).astype(jnp.bfloat16)
        for step, part in enumerate((part_0, part_1, part_2, part_3)):
            first = (blk_index // 4 - step & 3) * 4
            part = jnp.concatenate([part[c] for c in range(4)], 1)
            rows = jnp.dot(pick, part, preferred_element_type=jnp.float32).astype(jnp.bfloat16)
            for c in range(4):
                of_c = rows[:, 128 * c : 128 * c + 128]
                first_pieces[pl.ds(pl.multiple_of((first + c) * cut, 16), cut), :] = of_c[:cut]
                last_pieces[pl.ds(pl.multiple_of((first + c) * rest, 16), rest), :] = of_c[cut:]


def slots_of_pieces(parts):
    rows = 8 * EARLY_PIECES
    shapes = [
        jax.ShapeDtypeStruct((GROUP * rows, 128), jnp.bfloat16),
        jax.ShapeDtypeStruct((GROUP * (128 - rows), 128), jnp.bfloat16),
    ]
    return pl.pallas_call(
        slots_kernel,
        out_shape=shapes * 2,
        in_specs=[VMEM] * 4,
        out_specs=[VMEM] * 4,
        compiler_params=ROOM,
        name="slots",
    )(*parts)


def products(pieces, rows_w, total):
    depth = rows_w.shape[0]
    step = max(n for n in range(128, 1025, 128) if depth % n == 0)
    total[...] = jnp.zeros_like(total)

    def body(n, carry):
        at = pl.ds(pl.multiple_of(n * step, 128), step)
        left = [piece[:, :, at].reshape(-1, step) for piece in pieces]
        total[...] += jnp.dot(
            jnp.concatenate(left, 0), rows_w[at, :], preferred_element_type=jnp.float32
        )
        return carry

    lax.fori_loop(0, depth // step, body, 0)


def ladder_early_kernel(*refs):
    products(refs[:-2], refs[-2], refs[-1])


def ladder_early(pieces, rows_w):
    shape = (EARLY_PIECES * PIECE, rows_w.shape[1])
    return pl.pallas_call(
        ladder_early_kernel,
        out_shape=jax.ShapeDtypeStruct(shape, jnp.float32),
        in_specs=[VMEM] * (len(pieces) + 1),
        out_specs=VMEM,
        compiler_params=ROOM,
        name="ladder_early",
    )(*pieces, rows_w)


def ladder_late_kernel(*refs):
    pieces = refs[:-5]
    rows_w, early, mine, other, total = refs[-5:]
    core, blk_index = lax.axis_index("slab"), lax.axis_index("blk")
    products(pieces, rows_w, total)

    def place(n, value):
        chip = chip_of(n, core, blk_index)

        @pl.when(chip // 8 == core)
        def _():
            mine[chip & 7] = value

        @pl.when(chip // 8 != core)
        def _():
            other[chip & 7] = value

    def of_early(n, carry):
        place(n, early[pl.ds(pl.multiple_of(n * PIECE, PIECE), PIECE), :])
        return carry

    def of_late(n, carry):
        place(n + EARLY_PIECES, total[pl.ds(pl.multiple_of(n * PIECE, PIECE), PIECE), :])
        return carry

    lax.fori_loop(0, EARLY_PIECES, of_early, 0)
    lax.fori_loop(0, 16 - EARLY_PIECES, of_late, 0)


def ladder_late(pieces, rows_w, early):
    out_columns = rows_w.shape[1]
    half = jax.ShapeDtypeStruct((8, PIECE, out_columns), jnp.float32)
    return pl.pallas_call(
        ladder_late_kernel,
        out_shape=[half, half],
        in_specs=[VMEM] * (len(pieces) + 2),
        out_specs=[VMEM, VMEM],
        scratch_shapes=[pltpu.VMEM(((16 - EARLY_PIECES) * PIECE, out_columns), jnp.float32)],
        compiler_params=ROOM,
        name="ladder_late",
    )(*pieces, rows_w, early)


def ladder_end_kernel(dims, mine, other, out, rows):
    out_columns = out.shape[1]
    column = lax.axis_index("blk") * out_columns
    column = column + lax.broadcasted_iota(jnp.int32, (1, out_columns), 1)
    block, c, d = column >> 12, column >> 6 & 63, column & 63
    size_first = jnp.where(block == 0, dims[0, 0], dims[1, 0])
    size_second = jnp.where(block == 0, dims[0, 1], dims[1, 1])
    keep = (c < size_first) & (d < size_second)

    def body(pair, carry):
        even = mine[2 * pair] + other[2 * pair]
        odd = mine[2 * pair + 1] + other[2 * pair + 1]
        both = jnp.concatenate([even[:56], even[56:] + odd[:8], odd[8:]], 0)
        rows[pl.ds(pl.multiple_of(pair * 120, 8), 120), :] = jnp.where(keep, both, 0.0)
        return carry

    lax.fori_loop(0, 4, body, 0)
    out[...] = rows[...].astype(jnp.bfloat16)


def ladder_end(block_dims, mine, other):
    shape = (480, mine.shape[2])
    return pl.pallas_call(
        ladder_end_kernel,
        out_shape=jax.ShapeDtypeStruct(shape, jnp.bfloat16),
        in_specs=[SMEM, VMEM, VMEM],
        out_specs=VMEM,
        scratch_shapes=[pltpu.VMEM(shape, jnp.float32)],
        compiler_params=ROOM,
        name="ladder_end",
    )(block_dims, mine, other)


def turn(pieces, group_width, start, spread, turned):
    wide = GROUP * group_width
    count = sum(piece.shape[0] for piece in pieces)
    rows, each = count * PIECE, 8 * count
    n = 0
    for piece in pieces:

        def body(i, carry, piece=piece, n=n):
            part = piece[i, :, pl.ds(start, wide)].astype(jnp.float32)
            for b in range(wide // 128):
                at = pl.multiple_of((b * count + n + i) * PIECE, PIECE)
                spread[pl.ds(at, PIECE), :] = part[:, 128 * b : 128 * b + 128]
            return carry

        lax.fori_loop(0, piece.shape[0], body, 0)
        n += piece.shape[0]
    spread[wide // 128 * rows : wide // 128 * rows + rows, :] = jnp.zeros((rows, 128), jnp.float32)

    def columns(pair, carry):
        for c in range(GROUP):
            lo = c * group_width
            base = lo // 128
            blocks = [base] if lo % 128 + BS <= 128 else [base, base + 1]
            halves = []
            for odd in range(2):
                window = [
                    spread[pl.ds(b * rows + 2 * pair + odd, each, stride=8), :] for b in blocks
                ]
                window = jnp.concatenate(window, 1)
                halves.append(window[:, lo % 128 : lo % 128 + BS])
            at = pl.ds(pl.multiple_of(pair * 128, 128), 128)
            turned[c * each : (c + 1) * each, at] = jnp.concatenate(halves, 1).astype(turned.dtype)
        return carry

    lax.fori_loop(0, 4, columns, 0)


def first_part(core, plane):
    return (core == 0) == (plane < 3)


def group_starts(width, least, core, plane):
    first = jnp.where(core == 0, plane, 0) * (GROUP * width)
    own = GROUP * width + plane * (GROUP * least)
    return pl.multiple_of(first, 128), pl.multiple_of(own, 128)


def cycle_early_kernel(width, least, *refs):
    pieces, (first, own, spread) = refs[:-3], refs[-3:]
    core, plane = lax.axis_index("slab"), lax.axis_index("blk") & 3
    first_start, own_start = group_starts(width, least, core, plane)

    @pl.when(first_part(core, plane))
    def _():
        turn(pieces, width, first_start, spread, first)

    @pl.when(core == 1)
    def _():
        turn(pieces, least, own_start, spread, own)


def cycle_early(width, least, pieces):
    count = sum(p.shape[0] for p in pieces)
    shape = jax.ShapeDtypeStruct((GROUP * 8 * count, 8 * BS), jnp.bfloat16)
    blocks = GROUP * max(width, least) // 128 + 1
    return pl.pallas_call(
        functools.partial(cycle_early_kernel, width, least),
        out_shape=[shape, shape],
        in_specs=[VMEM] * len(pieces),
        out_specs=[VMEM, VMEM],
        scratch_shapes=[pltpu.VMEM((blocks * count * PIECE, 128), jnp.float32)],
        compiler_params=ROOM,
        name="cycle_early",
    )(*pieces)


def cycle_late_kernel(width, least, *refs):
    pieces, refs = refs[:-10], refs[-10:]
    turned_first, turned_own, slots_first, late_first, slots_own, late_own, first, own = refs[:8]
    spread, turned = refs[8:]
    core, plane = lax.axis_index("slab"), lax.axis_index("blk") & 3
    first_start, own_start = group_starts(width, least, core, plane)

    def total(slots, early, slots_late, out):
        pairs = ((slots, early), (slots_late, turned))
        out[...] = sum(
            lax.dot_general(
                left[...], right[...], (((0,), (0,)), ((), ())), preferred_element_type=jnp.float32
            )
            for left, right in pairs
        )

    first[...] = jnp.zeros_like(first)
    own[...] = jnp.zeros_like(own)

    @pl.when(first_part(core, plane))
    def _():
        turn(pieces, width, first_start, spread, turned)
        total(slots_first, turned_first, late_first, first)

    @pl.when(core == 1)
    def _():
        turn(pieces, least, own_start, spread, turned)
        total(slots_own, turned_own, late_own, own)


def cycle_late(width, least, pieces, turned, slots_first, slots_own):
    count = sum(p.shape[0] for p in pieces)
    shape = jax.ShapeDtypeStruct((128, 8 * BS), jnp.float32)
    blocks = GROUP * max(width, least) // 128 + 1
    return pl.pallas_call(
        functools.partial(cycle_late_kernel, width, least),
        out_shape=[shape, shape],
        in_specs=[VMEM] * (6 + len(pieces)),
        out_specs=[VMEM, VMEM],
        scratch_shapes=[
            pltpu.VMEM((blocks * count * PIECE, 128), jnp.float32),
            pltpu.VMEM((GROUP * 8 * count, 8 * BS), jnp.bfloat16),
        ],
        compiler_params=ROOM,
        name="cycle_late",
    )(*pieces, *turned, *slots_first, *slots_own)


def after(value, *others):
    return lax.optimization_barrier((value,) + others)[0]


def compacted(width, least, amplitudes, ladder_ints, cycle_ints, block_dims, moved, moved_ints):
    core = lax.axis_index("slab")
    blk_index = lax.axis_index("blk")
    plane, z = blk_index % 4, blk_index // 4
    wide_columns, narrow_columns = GROUP * width, GROUP * least
    columns = max(3 * wide_columns, wide_columns + 4 * narrow_columns)

    own = prep(width, least, columns, block_dims, amplitudes, moved)[None]
    near = [send(own, up(step)) for step in (1, 3)]
    plane_1 = send(own, first_axis)
    plane_2 = send(own, second_axis)
    moved_ints = to_other_core(after(moved_ints, own), (0,))
    plane_12 = send(plane_1, second_axis)
    rows_w = compact_rows(ladder_ints, moved_ints, width, least, columns, core)
    near = after(jnp.concatenate(near), plane_1, plane_2)
    far = send(after(own, near), up(2))
    near_1 = send(near, first_axis)
    near_2 = send(near, second_axis)
    near_12 = send(near_1, second_axis)
    far_1 = send(far, first_axis)
    far_2 = send(far, second_axis)
    far_12 = send(far_1, second_axis)
    shares = after(cycle_ints[0], far)

    def share(step):
        part = lax.dynamic_slice_in_dim(shares, (z + step) % 4 * 128, 128, 2)
        return send(part, up(step)) if step else part

    slots = slots_of_pieces([share(step) for step in range(4)])
    slots_first = [
        jnp.where(core == 0, here, to_other_core(there, (0,)))
        for here, there in zip(slots[:2], slots[2:])
    ]

    out_columns = ladder_ints.shape[1]
    pieces = [own, plane_1, plane_2, plane_12, near, near_1, near_2]
    last = [near_12, far, far_1, far_2, far_12]
    sums = ladder_early(pieces, rows_w)
    turned = cycle_early(width, least, pieces)
    terms = cycle_late(width, least, last, turned, slots_first, slots[:2])
    pairs = [(2 * chip + 1, 2 * chip) for chip in (3, 7, 11, 15)]
    last_group = lax.ppermute(terms[0], AXES, pairs)
    mine, other = ladder_late(last, rows_w, after(sums, terms[0]))
    other = to_other_core(other, (0, 1))
    term = jnp.where(core == 0, jnp.where(plane == 3, last_group, terms[0]), terms[1])
    term = term.reshape(4, 32, 8 * BS)

    def chunk(chip):
        return lax.dynamic_index_in_dim(term, chip, 0, False)

    cycle_sum = chunk(plane)
    for distance, target in ((1, along_x), (2, along_y), (3, across)):
        cycle_sum = cycle_sum + send(chunk(plane ^ distance), target)
    ladder_res = ladder_end(block_dims, mine, other)
    allowed = cycle_allowed(block_dims, core, blk_index, 32, 8 * BS)
    cycle_res = jnp.where(allowed, cycle_sum, 0.0).astype(jnp.bfloat16)[None]
    return (ladder_res, cycle_res)


WIDTHS = (48, 56, 64)


def local(amplitudes, ladder_ints, cycle_ints, block_dims):
    moved = to_other_core(amplitudes, (0,))
    moved_ints = ladder_ints.reshape(4, 4, 4 * BS, -1)[:, 3].reshape(GROUP * BS, -1)
    size = block_dims[0, 1]

    def choose(widths):
        if len(widths) == 1:
            return functools.partial(compacted, widths[0], LEAST)
        half = len(widths) // 2
        fewer, more = choose(widths[:half]), choose(widths[half:])
        return lambda *given: lax.cond(size <= widths[half - 1], fewer, more, *given)

    return lax.cond(
        block_dims[1, 1] <= LEAST,
        choose(WIDTHS),
        functools.partial(compacted, BS, BS),
        amplitudes,
        ladder_ints,
        cycle_ints,
        block_dims,
        moved,
        moved_ints,
    )


def solution(mesh):
    in_specs = (P("blk", "slab"), P("slab", "blk"), P("slab", "blk", None, None), P())
    out_specs = (P("slab", "blk"), P("slab", "blk", None))
    body = local if dict(mesh.shape) == {"blk": 16, "slab": 2} else plain
    return jax.shard_map(body, mesh=mesh, in_specs=in_specs, out_specs=out_specs, check_vma=False)
```

```python
import functools

import jax
import jax.numpy as jnp
import numpy as np
from jax import lax
from jax.experimental import pallas as pl
from jax.experimental.pallas import tpu as pltpu
from jax.sharding import PartitionSpec as P

BS = 64
LEAST = 24
GROUP = 16
PIECE = 64
AXES = ("blk", "slab")


def block_sizes(block_dims, owner):
    blocks_count = block_dims.shape[0]
    select = owner[:, None] == lax.iota(jnp.int32, blocks_count)[None, :]
    size_first = jnp.sum(jnp.where(select, block_dims[None, :, 0], 0), 1)
    size_second = jnp.sum(jnp.where(select, block_dims[None, :, 1], 0), 1)
    return (size_first, size_second)


def column_valid(block_dims, first_column, column_count):
    column = first_column + lax.iota(jnp.int32, column_count)
    owner = column // (BS * BS)
    size_first, size_second = block_sizes(block_dims, owner)
    return (column // BS % BS < size_first) & (column % BS < size_second)


def cycle_allowed(block_dims, slab_index, blk_index, local_rows, columns):
    own_block = jnp.full((1,), slab_index, jnp.int32)
    size_first, size_second = block_sizes(block_dims, own_block)
    row_virtual = (blk_index * local_rows + lax.iota(jnp.int32, local_rows)) % BS
    column_virtual = lax.iota(jnp.int32, columns) % BS
    return (row_virtual[:, None] < size_first[0]) & (column_virtual[None, :] < size_second[0])


def plain(amplitudes, ladder_ints, cycle_ints, block_dims):
    slab_index = lax.axis_index("slab")
    blk_index = lax.axis_index("blk")
    block_width = amplitudes.shape[1]
    valid = column_valid(block_dims, slab_index * block_width, block_width)
    masked = jnp.where(valid[None, :], amplitudes, jnp.zeros((), amplitudes.dtype))
    gathered = lax.all_gather(masked, "blk", axis=0, tiled=True)
    pair_rows = gathered.shape[0]
    ladder_sum = lax.psum_scatter(
        jnp.dot(gathered, ladder_ints, preferred_element_type=jnp.float32),
        "slab",
        scatter_dimension=0,
        tiled=True,
    )
    out_columns = ladder_ints.shape[1]
    out_valid = column_valid(block_dims, blk_index * out_columns, out_columns)
    ladder_res = jnp.where(out_valid[None, :], ladder_sum, 0.0).astype(jnp.bfloat16)
    occupied = cycle_ints.shape[2]
    j_window = pair_rows // occupied
    columns = lax.all_to_all(masked, "blk", split_axis=1, concat_axis=0, tiled=True)
    c_part = cycle_ints.shape[1]
    amp_part = columns.reshape(occupied, j_window, c_part, BS)
    cycle_term = jnp.einsum(
        "cke,kjcd->ejd", cycle_ints[0], amp_part, preferred_element_type=jnp.float32
    )
    cycle_term = cycle_term.reshape(cycle_term.shape[0], j_window * BS)
    cycle_sum = lax.psum_scatter(cycle_term, "blk", scatter_dimension=0, tiled=True)
    allowed = cycle_allowed(block_dims, slab_index, blk_index, cycle_sum.shape[0], j_window * BS)
    cycle_res = jnp.where(allowed, cycle_sum, 0.0).astype(jnp.bfloat16)[None]
    return (ladder_res, cycle_res)


def send(value, target, cores=(0, 1)):
    pairs = []
    for chip in range(16):
        for core in cores:
            x, y, z = target(chip & 1, chip >> 1 & 1, chip >> 2, core)
            pairs.append((2 * chip + core, 2 * (4 * (z % 4) + 2 * y + x) + core))
    return lax.ppermute(value, AXES, pairs)


def along_x(x, y, z, core):
    return (1 - x, y, z)


def along_y(x, y, z, core):
    return (x, 1 - y, z)


def across(x, y, z, core):
    return (1 - x, 1 - y, z)


def first_axis(x, y, z, core):
    return along_x(x, y, z, core) if core == 0 else along_y(x, y, z, core)


def second_axis(x, y, z, core):
    return along_y(x, y, z, core) if core == 0 else along_x(x, y, z, core)


def up(step):
    return lambda x, y, z, core: (x, y, z + step)


def to_other_core(value, cores):
    return lax.ppermute(value, "slab", [(core, 1 - core) for core in cores])


def compact_tables(width):
    column = np.arange(GROUP * width)
    c, d = column // width, column % width
    return np.stack([c * BS + d, c // 4 * GROUP + c % 4, d] + [c * 0] * 5).astype(np.int32)


def prep_kernel(width, least, dims, amp, moved, wide, narrow, out, rows):
    def tiles(table, group_width):
        result = []
        for lo in range(0, GROUP * group_width, 128):
            start = lo // group_width // 2 * 128
            stop = -(-((lo + 127) // group_width + 1) // 2) * 128
            source = table[0:1, lo : lo + 128] - start
            at = lax.broadcasted_iota(jnp.int32, (stop - start, 128), 0)
            pick = jnp.where(at == source, 1.0, 0.0).astype(jnp.bfloat16)
            result.append((lo, start, stop, pick))
        return result

    def compact(source, group, table, picks, block, to):
        def part(at):
            column = at // (4 * BS) * (GROUP * BS) + group * (4 * BS) + at % (4 * BS)
            return source[:, column : column + 128]

        for lo, start, stop, pick in picks:
            window = jnp.concatenate([part(at) for at in range(start, stop, 128)], 1)
            value = jnp.dot(window, pick, preferred_element_type=jnp.float32)
            c, d = table[1:2, lo : lo + 128] + 4 * group, table[2:3, lo : lo + 128]
            keep = (c < dims[block, 0]) & (d < dims[block, 1])
            rows[0:60, to + lo : to + lo + 128] = jnp.where(keep, value, 0.0).astype(jnp.bfloat16)

    core, shift = lax.axis_index("slab"), lax.axis_index("blk") % 2 * 4
    wide_columns, narrow_columns = GROUP * width, GROUP * least
    rows[...] = jnp.zeros_like(rows)

    @pl.when(core == 0)
    def _():
        picks = tiles(wide, width)
        for g in range(3):
            compact(amp, g, wide, picks, 0, g * wide_columns)

    @pl.when(core == 1)
    def _():
        compact(moved, 3, wide, tiles(wide, width), 0, 0)
        picks = tiles(narrow, least)
        for g in range(4):
            compact(amp, g, narrow, picks, 1, wide_columns + g * narrow_columns)

    shape = (PIECE, PIECE)
    down = lax.broadcasted_iota(jnp.int32, shape, 0) - lax.broadcasted_iota(jnp.int32, shape, 1)
    down = jnp.where(down == shift, 1.0, 0.0).astype(jnp.bfloat16)
    out[...] = jnp.dot(down, rows[...], preferred_element_type=jnp.float32).astype(jnp.bfloat16)


def prep(width, least, columns, block_dims, amplitudes, moved):
    smem = pl.BlockSpec(memory_space=pltpu.SMEM)
    vmem = pl.BlockSpec(memory_space=pltpu.VMEM)
    return pl.pallas_call(
        functools.partial(prep_kernel, width, least),
        out_shape=jax.ShapeDtypeStruct((PIECE, columns), jnp.bfloat16),
        in_specs=[smem] + [vmem] * 4,
        out_specs=vmem,
        scratch_shapes=[pltpu.VMEM((PIECE, columns), jnp.bfloat16)],
        name="prep",
    )(
        block_dims,
        amplitudes,
        moved,
        jnp.asarray(compact_tables(width)),
        jnp.asarray(compact_tables(least)),
    )


def compact_rows(ladder_ints, moved_ints, width, least, columns, core):
    def pad(rows):
        return jnp.pad(rows, ((0, columns - rows.shape[0]), (0, 0)))

    out_columns = ladder_ints.shape[1]

    def cut(rows, keep):
        rows = rows.reshape(4, -1, 4, BS, out_columns)[:, :, :, :keep]
        return rows.transpose(1, 0, 2, 3, 4).reshape(-1, out_columns)

    def of_first():
        groups = ladder_ints.reshape(4, 4, 4 * BS, out_columns)
        return pad(cut(groups[:, :3], width))

    def of_second():
        return pad(jnp.concatenate([cut(moved_ints, width), cut(ladder_ints, least)]))

    return lax.cond(core == 0, of_first, of_second)


def distance_of(slot, core):
    swapped = (slot & 1) * 2 + (slot >> 1)
    return jnp.where(core == 0, slot, swapped)


def chip_of(n, core, blk_index):
    near = (n >= 4) & (n < 12)
    z_step = jnp.where(near, (n & 1) * 2 + 1, jnp.where(n < 4, 0, 2))
    slot = jnp.where(near, (n - 4) >> 1, n & 3)
    z = (blk_index // 4 - z_step) & 3
    return z * 4 + ((blk_index & 3) ^ distance_of(slot, core))


VMEM = pl.BlockSpec(memory_space=pltpu.VMEM)
SMEM = pl.BlockSpec(memory_space=pltpu.SMEM)
ROOM = pltpu.CompilerParams(vmem_limit_bytes=48 * 1024 * 1024)
STAGES = (10, 4, 2)


def slots_kernel(part_0, part_1, part_2, part_3, here, there):
    core, blk_index = lax.axis_index("slab"), lax.axis_index("blk")
    occupied = part_0.shape[1]
    slot = lax.broadcasted_iota(jnp.int32, (128, 1), 0)
    at = lax.broadcasted_iota(jnp.int32, (128, occupied), 1)
    for order, out in ((core, here), (1 - core, there)):
        chip = chip_of(slot >> 3, order, blk_index)
        k = 15 * (chip >> 1) + 7 * (chip & 1) + (slot & 7)
        pick = jnp.where(at == k, 1.0, 0.0).astype(jnp.bfloat16)
        for step, part in enumerate((part_0, part_1, part_2, part_3)):
            first = (blk_index // 4 - step & 3) * 4
            part = jnp.concatenate([part[c] for c in range(4)], 1)
            rows = jnp.dot(pick, part, preferred_element_type=jnp.float32).astype(jnp.bfloat16)
            for c in range(4):
                lo = 0
                for stage in STAGES:
                    each = 8 * stage
                    to = pl.multiple_of(GROUP * lo + (first + c) * each, 16)
                    out[pl.ds(to, each), :] = rows[lo : lo + each, 128 * c : 128 * c + 128]
                    lo += each


def slots_of_pieces(parts):
    shape = jax.ShapeDtypeStruct((GROUP * 128, 128), jnp.bfloat16)
    return pl.pallas_call(
        slots_kernel,
        out_shape=[shape, shape],
        in_specs=[VMEM] * 4,
        out_specs=[VMEM] * 2,
        compiler_params=ROOM,
        name="slots",
    )(*parts)


def products(pieces, rows_w, total):
    depth = rows_w.shape[0]
    step = max(n for n in range(128, 1025, 128) if depth % n == 0)
    total[...] = jnp.zeros_like(total)

    def body(n, carry):
        at = pl.ds(pl.multiple_of(n * step, 128), step)
        left = [piece[:, :, at].reshape(-1, step) for piece in pieces]
        total[...] += jnp.dot(
            jnp.concatenate(left, 0), rows_w[at, :], preferred_element_type=jnp.float32
        )
        return carry

    lax.fori_loop(0, depth // step, body, 0)


def ladder_part_kernel(*refs):
    products(refs[:-2], refs[-2], refs[-1])


def ladder_part(pieces, rows_w):
    count = sum(piece.shape[0] for piece in pieces)
    shape = (count * PIECE, rows_w.shape[1])
    return pl.pallas_call(
        ladder_part_kernel,
        out_shape=jax.ShapeDtypeStruct(shape, jnp.float32),
        in_specs=[VMEM] * (len(pieces) + 1),
        out_specs=VMEM,
        compiler_params=ROOM,
        name="ladder_part",
    )(*pieces, rows_w)


def ladder_late_kernel(*refs):
    pieces = refs[:-6]
    rows_w, early, middle, mine, other, total = refs[-6:]
    core, blk_index = lax.axis_index("slab"), lax.axis_index("blk")
    products(pieces, rows_w, total)

    def place(first, sums):
        def body(n, carry):
            chip = chip_of(first + n, core, blk_index)
            value = sums[pl.ds(pl.multiple_of(n * PIECE, PIECE), PIECE), :]

            @pl.when(chip // 8 == core)
            def _():
                mine[chip & 7] = value

            @pl.when(chip // 8 != core)
            def _():
                other[chip & 7] = value

            return carry

        lax.fori_loop(0, sums.shape[0] // PIECE, body, 0)

    place(0, early)
    place(STAGES[0], middle)
    place(STAGES[0] + STAGES[1], total)


def ladder_late(pieces, rows_w, early, middle):
    out_columns = rows_w.shape[1]
    half = jax.ShapeDtypeStruct((8, PIECE, out_columns), jnp.float32)
    return pl.pallas_call(
        ladder_late_kernel,
        out_shape=[half, half],
        in_specs=[VMEM] * (len(pieces) + 3),
        out_specs=[VMEM, VMEM],
        scratch_shapes=[pltpu.VMEM((STAGES[2] * PIECE, out_columns), jnp.float32)],
        compiler_params=ROOM,
        name="ladder_late",
    )(*pieces, rows_w, early, middle)


def ladder_end_kernel(dims, mine, other, out, rows):
    out_columns = out.shape[1]
    column = lax.axis_index("blk") * out_columns
    column = column + lax.broadcasted_iota(jnp.int32, (1, out_columns), 1)
    block, c, d = column >> 12, column >> 6 & 63, column & 63
    size_first = jnp.where(block == 0, dims[0, 0], dims[1, 0])
    size_second = jnp.where(block == 0, dims[0, 1], dims[1, 1])
    keep = (c < size_first) & (d < size_second)

    def body(pair, carry):
        even = mine[2 * pair] + other[2 * pair]
        odd = mine[2 * pair + 1] + other[2 * pair + 1]
        both = jnp.concatenate([even[:56], even[56:] + odd[:8], odd[8:]], 0)
        rows[pl.ds(pl.multiple_of(pair * 120, 8), 120), :] = jnp.where(keep, both, 0.0)
        return carry

    lax.fori_loop(0, 4, body, 0)
    out[...] = rows[...].astype(jnp.bfloat16)


def ladder_end(block_dims, mine, other):
    shape = (480, mine.shape[2])
    return pl.pallas_call(
        ladder_end_kernel,
        out_shape=jax.ShapeDtypeStruct(shape, jnp.bfloat16),
        in_specs=[SMEM, VMEM, VMEM],
        out_specs=VMEM,
        scratch_shapes=[pltpu.VMEM(shape, jnp.float32)],
        compiler_params=ROOM,
        name="ladder_end",
    )(block_dims, mine, other)


def turn(pieces, group_width, start, spread, turned):
    wide = GROUP * group_width
    count = sum(piece.shape[0] for piece in pieces)
    rows, each = count * PIECE, 8 * count
    n = 0
    for piece in pieces:

        def body(i, carry, piece=piece, n=n):
            part = piece[i, :, pl.ds(start, wide)].astype(jnp.float32)
            for b in range(wide // 128):
                at = pl.multiple_of((b * count + n + i) * PIECE, PIECE)
                spread[pl.ds(at, PIECE), :] = part[:, 128 * b : 128 * b + 128]
            return carry

        lax.fori_loop(0, piece.shape[0], body, 0)
        n += piece.shape[0]
    spread[wide // 128 * rows : wide // 128 * rows + rows, :] = jnp.zeros((rows, 128), jnp.float32)

    def columns(pair, carry):
        for c in range(GROUP):
            lo = c * group_width
            base = lo // 128
            blocks = [base] if lo % 128 + BS <= 128 else [base, base + 1]
            halves = []
            for odd in range(2):
                window = [
                    spread[pl.ds(b * rows + 2 * pair + odd, each, stride=8), :] for b in blocks
                ]
                window = jnp.concatenate(window, 1)
                halves.append(window[:, lo % 128 : lo % 128 + BS])
            at = pl.ds(pl.multiple_of(pair * 128, 128), 128)
            turned[c * each : (c + 1) * each, at] = jnp.concatenate(halves, 1).astype(turned.dtype)
        return carry

    lax.fori_loop(0, 4, columns, 0)


def first_part(core, plane):
    return (core == 0) == (plane < 3)


def group_starts(width, least, core, plane):
    first = jnp.where(core == 0, plane, 0) * (GROUP * width)
    own = GROUP * width + plane * (GROUP * least)
    return pl.multiple_of(first, 128), pl.multiple_of(own, 128)


def cycle_early_kernel(width, least, *refs):
    pieces, (first, own, spread) = refs[:-3], refs[-3:]
    core, plane = lax.axis_index("slab"), lax.axis_index("blk") & 3
    first_start, own_start = group_starts(width, least, core, plane)

    @pl.when(first_part(core, plane))
    def _():
        turn(pieces, width, first_start, spread, first)

    @pl.when(core == 1)
    def _():
        turn(pieces, least, own_start, spread, own)


def cycle_early(width, least, pieces):
    count = sum(p.shape[0] for p in pieces)
    shape = jax.ShapeDtypeStruct((GROUP * 8 * count, 8 * BS), jnp.bfloat16)
    blocks = GROUP * max(width, least) // 128 + 1
    return pl.pallas_call(
        functools.partial(cycle_early_kernel, width, least),
        out_shape=[shape, shape],
        in_specs=[VMEM] * len(pieces),
        out_specs=[VMEM, VMEM],
        scratch_shapes=[pltpu.VMEM((blocks * count * PIECE, 128), jnp.float32)],
        compiler_params=ROOM,
        name="cycle_early",
    )(*pieces)


def cycle_sum_kernel(width, least, row, turned_before, *refs):
    pieces, refs = refs[:-8], refs[-8:]
    before_first, before_own, slots_first, slots_own, first, own, spread, turned = refs
    core, plane = lax.axis_index("slab"), lax.axis_index("blk") & 3
    first_start, own_start = group_starts(width, least, core, plane)

    def add(slots, row, right):
        return lax.dot_general(
            slots[row : row + right.shape[0], :],
            right[...],
            (((0,), (0,)), ((), ())),
            preferred_element_type=jnp.float32,
        )

    def total(group_width, start, slots, before, out):
        turn(pieces, group_width, start, spread, turned)
        if turned_before:
            out[...] = add(slots, 0, before) + add(slots, row, turned)
        else:
            out[...] = before[...] + add(slots, row, turned)

    first[...] = jnp.zeros_like(first)
    own[...] = jnp.zeros_like(own)

    @pl.when(first_part(core, plane))
    def _():
        total(width, first_start, slots_first, before_first, first)

    @pl.when(core == 1)
    def _():
        total(least, own_start, slots_own, before_own, own)


def cycle_add(width, least, stage, pieces, before, slots_first, slots_own):
    count = STAGES[stage]
    shape = jax.ShapeDtypeStruct((128, 8 * BS), jnp.float32)
    blocks = GROUP * max(width, least) // 128 + 1
    row = GROUP * 8 * sum(STAGES[:stage])
    turned_before = before[0].dtype == jnp.bfloat16
    return pl.pallas_call(
        functools.partial(cycle_sum_kernel, width, least, row, turned_before),
        out_shape=[shape, shape],
        in_specs=[VMEM] * (4 + len(pieces)),
        out_specs=[VMEM, VMEM],
        scratch_shapes=[
            pltpu.VMEM((blocks * count * PIECE, 128), jnp.float32),
            pltpu.VMEM((GROUP * 8 * count, 8 * BS), jnp.bfloat16),
        ],
        compiler_params=ROOM,
        name="cycle_sum",
    )(*pieces, *before, slots_first, slots_own)


def together(*values):
    return lax.optimization_barrier(values)


def after(value, *others):
    return together(value, *others)[0]


def compacted(width, least, amplitudes, ladder_ints, cycle_ints, block_dims, moved):
    core = lax.axis_index("slab")
    blk_index = lax.axis_index("blk")
    plane, z = blk_index % 4, blk_index // 4
    wide_columns, narrow_columns = GROUP * width, GROUP * least
    columns = max(3 * wide_columns, wide_columns + 4 * narrow_columns)

    own = prep(width, least, columns, block_dims, amplitudes, moved)[None]
    near = [send(own, up(step)) for step in (1, 3)]
    plane_1 = send(own, first_axis)
    plane_2 = send(own, second_axis)
    plane_12 = send(plane_1, second_axis)
    ints, shares = together(ladder_ints, cycle_ints[0], own)[:2]
    moved_ints = ints.reshape(4, 4, 4 * BS, -1)[:, 3].reshape(GROUP * BS, -1)
    shares = [lax.dynamic_slice_in_dim(shares, (z + step) % 4 * 128, 128, 2) for step in range(4)]
    near, far, moved_ints, ints, *shares = together(
        jnp.concatenate(near), own, moved_ints, ints, *shares, plane_1, plane_2, plane_12
    )[:8]
    far = send(far, up(2))
    near_1 = send(near, first_axis)
    near_2 = send(near, second_axis)
    moved_ints = to_other_core(moved_ints, (0,))
    far, near_1, near_2, moved_ints, *shares = together(far, near_1, near_2, moved_ints, *shares)
    far_1 = send(far, first_axis)
    far_2 = send(far, second_axis)
    near_12 = send(near_1, second_axis)
    shares[3] = send(shares[3], up(3))
    shares[2] = send(shares[2], up(2))
    shares[1] = send(after(shares[1], shares[3]), up(1))
    rows_w = compact_rows(ints, moved_ints, width, least, columns, core)
    early = [own, plane_1, plane_2, plane_12, near, near_1, near_2]
    sums = ladder_part(early, rows_w)
    turned = cycle_early(width, least, early)
    far_1, far_2, near_12, sums, turned, *shares = together(
        far_1, far_2, near_12, sums, turned, *shares
    )
    far_12 = send(far_1, second_axis)
    slots, there = slots_of_pieces(shares)
    slots_first = jnp.where(core == 0, slots, to_other_core(there, (0,)))
    middle = [near_12, far, far_1]
    sums_middle = ladder_part(middle, rows_w)
    terms = cycle_add(width, least, 1, middle, turned, slots_first, slots)

    late = [far_2, far_12]
    terms = cycle_add(width, least, 2, late, terms, slots_first, slots)
    pairs = [(2 * chip + 1, 2 * chip) for chip in (3, 7, 11, 15)]
    last_group = lax.ppermute(terms[0], AXES, pairs)
    mine, other = ladder_late(late, rows_w, after(sums, terms[0]), sums_middle)
    other = to_other_core(other, (0, 1))
    term = jnp.where(core == 0, jnp.where(plane == 3, last_group, terms[0]), terms[1])
    term = term.reshape(4, 32, 8 * BS)

    def chunk(chip):
        return lax.dynamic_index_in_dim(term, chip, 0, False)

    cycle_sum = chunk(plane)
    for distance, target in ((1, along_x), (2, along_y), (3, across)):
        cycle_sum = cycle_sum + send(chunk(plane ^ distance), target)
    ladder_res = ladder_end(block_dims, mine, other)
    allowed = cycle_allowed(block_dims, core, blk_index, 32, 8 * BS)
    cycle_res = jnp.where(allowed, cycle_sum, 0.0).astype(jnp.bfloat16)[None]
    return (ladder_res, cycle_res)


WIDTHS = (48, 56, 64)


def local(amplitudes, ladder_ints, cycle_ints, block_dims):
    moved = to_other_core(amplitudes, (0,))
    fits = [block_dims[0, 1] > width for width in WIDTHS[:-1]]
    choice = sum(fit.astype(jnp.int32) for fit in fits)
    choice = jnp.where(block_dims[1, 1] <= LEAST, choice, len(WIDTHS))
    branches = [functools.partial(compacted, width, LEAST) for width in WIDTHS]
    branches.append(functools.partial(compacted, BS, BS))
    return lax.switch(
        choice, branches, amplitudes, ladder_ints, cycle_ints, block_dims, moved
    )


def solution(mesh):
    in_specs = (P("blk", "slab"), P("slab", "blk"), P("slab", "blk", None, None), P())
    out_specs = (P("slab", "blk"), P("slab", "blk", None))
    body = local if dict(mesh.shape) == {"blk": 16, "slab": 2} else plain
    return jax.shard_map(body, mesh=mesh, in_specs=in_specs, out_specs=out_specs, check_vma=False)
```

```python
import functools

import jax
import jax.numpy as jnp
import numpy as np
from jax import lax
from jax.experimental import pallas as pl
from jax.experimental.pallas import tpu as pltpu
from jax.sharding import PartitionSpec as P

BS = 64
LEAST = 24
GROUP = 16
PIECE = 64
AXES = ("blk", "slab")


def block_sizes(block_dims, owner):
    blocks_count = block_dims.shape[0]
    select = owner[:, None] == lax.iota(jnp.int32, blocks_count)[None, :]
    size_first = jnp.sum(jnp.where(select, block_dims[None, :, 0], 0), 1)
    size_second = jnp.sum(jnp.where(select, block_dims[None, :, 1], 0), 1)
    return (size_first, size_second)


def column_valid(block_dims, first_column, column_count):
    column = first_column + lax.iota(jnp.int32, column_count)
    owner = column // (BS * BS)
    size_first, size_second = block_sizes(block_dims, owner)
    return (column // BS % BS < size_first) & (column % BS < size_second)


def plain(amplitudes, ladder_ints, cycle_ints, block_dims):
    slab_index = lax.axis_index("slab")
    blk_index = lax.axis_index("blk")
    block_width = amplitudes.shape[1]
    valid = column_valid(block_dims, slab_index * block_width, block_width)
    masked = jnp.where(valid[None, :], amplitudes, jnp.zeros((), amplitudes.dtype))
    gathered = lax.all_gather(masked, "blk", axis=0, tiled=True)
    pair_rows = gathered.shape[0]
    ladder_sum = lax.psum_scatter(
        jnp.dot(gathered, ladder_ints, preferred_element_type=jnp.float32),
        "slab",
        scatter_dimension=0,
        tiled=True,
    )
    out_columns = ladder_ints.shape[1]
    out_valid = column_valid(block_dims, blk_index * out_columns, out_columns)
    ladder_res = jnp.where(out_valid[None, :], ladder_sum, 0.0).astype(jnp.bfloat16)
    occupied = cycle_ints.shape[2]
    j_window = pair_rows // occupied
    columns = lax.all_to_all(masked, "blk", split_axis=1, concat_axis=0, tiled=True)
    c_part = cycle_ints.shape[1]
    amp_part = columns.reshape(occupied, j_window, c_part, BS)
    cycle_term = jnp.einsum(
        "cke,kjcd->ejd", cycle_ints[0], amp_part, preferred_element_type=jnp.float32
    )
    cycle_term = cycle_term.reshape(cycle_term.shape[0], j_window * BS)
    cycle_sum = lax.psum_scatter(cycle_term, "blk", scatter_dimension=0, tiled=True)
    own_block = jnp.full((1,), slab_index, jnp.int32)
    size_first, size_second = block_sizes(block_dims, own_block)
    local_rows = cycle_sum.shape[0]
    row_virtual = (blk_index * local_rows + lax.iota(jnp.int32, local_rows)) % BS
    column_virtual = lax.iota(jnp.int32, j_window * BS) % BS
    allowed = (row_virtual[:, None] < size_first[0]) & (column_virtual[None, :] < size_second[0])
    cycle_res = jnp.where(allowed, cycle_sum, 0.0).astype(jnp.bfloat16)[None]
    return (ladder_res, cycle_res)


def send(value, target, cores=(0, 1)):
    pairs = []
    for chip in range(16):
        for core in cores:
            x, y, z = target(chip & 1, chip >> 1 & 1, chip >> 2, core)
            pairs.append((2 * chip + core, 2 * (4 * (z % 4) + 2 * y + x) + core))
    return lax.ppermute(value, AXES, pairs)


def along_x(x, y, z, core):
    return (1 - x, y, z)


def along_y(x, y, z, core):
    return (x, 1 - y, z)


def across(x, y, z, core):
    return (1 - x, 1 - y, z)


def first_axis(x, y, z, core):
    return along_x(x, y, z, core) if core == 0 else along_y(x, y, z, core)


def second_axis(x, y, z, core):
    return along_y(x, y, z, core) if core == 0 else along_x(x, y, z, core)


def up(step):
    return lambda x, y, z, core: (x, y, z + step)


def to_other_core(value, cores):
    return lax.ppermute(value, "slab", [(core, 1 - core) for core in cores])


def compact_tables(width):
    column = np.arange(GROUP * width)
    c, d = column // width, column % width
    return np.stack([c * BS + d, c // 4 * GROUP + c % 4, d] + [c * 0] * 5).astype(np.int32)


def prep_kernel(width, least, dims, amp, moved, wide, narrow, out, rows):
    def tiles(table, group_width):
        result = []
        for lo in range(0, GROUP * group_width, 128):
            start = lo // group_width // 2 * 128
            stop = -(-((lo + 127) // group_width + 1) // 2) * 128
            source = table[0:1, lo : lo + 128] - start
            at = lax.broadcasted_iota(jnp.int32, (stop - start, 128), 0)
            pick = jnp.where(at == source, 1.0, 0.0).astype(jnp.bfloat16)
            result.append((lo, start, stop, pick))
        return result

    def compact(source, group, table, picks, block, to):
        def part(at):
            column = at // (4 * BS) * (GROUP * BS) + group * (4 * BS) + at % (4 * BS)
            return source[:, column : column + 128]

        for lo, start, stop, pick in picks:
            window = jnp.concatenate([part(at) for at in range(start, stop, 128)], 1)
            value = jnp.dot(window, pick, preferred_element_type=jnp.float32)
            c, d = table[1:2, lo : lo + 128] + 4 * group, table[2:3, lo : lo + 128]
            keep = (c < dims[block, 0]) & (d < dims[block, 1])
            rows[0:60, to + lo : to + lo + 128] = jnp.where(keep, value, 0.0).astype(jnp.bfloat16)

    core, shift = lax.axis_index("slab"), lax.axis_index("blk") % 2 * 4
    wide_columns, narrow_columns = GROUP * width, GROUP * least
    rows[...] = jnp.zeros_like(rows)

    @pl.when(core == 0)
    def _():
        picks = tiles(wide, width)
        for g in range(3):
            compact(amp, g, wide, picks, 0, g * wide_columns)

    @pl.when(core == 1)
    def _():
        picks = tiles(narrow, least)
        for g in range(4):
            compact(amp, g, narrow, picks, 1, g * narrow_columns)
        compact(moved, 3, wide, tiles(wide, width), 0, 4 * narrow_columns)

    shape = (PIECE, PIECE)
    down = lax.broadcasted_iota(jnp.int32, shape, 0) - lax.broadcasted_iota(jnp.int32, shape, 1)
    down = jnp.where(down == shift, 1.0, 0.0).astype(jnp.bfloat16)
    out[...] = jnp.dot(down, rows[...], preferred_element_type=jnp.float32).astype(jnp.bfloat16)


def prep(width, least, columns, block_dims, amplitudes, moved):
    smem = pl.BlockSpec(memory_space=pltpu.SMEM)
    vmem = pl.BlockSpec(memory_space=pltpu.VMEM)
    return pl.pallas_call(
        functools.partial(prep_kernel, width, least),
        out_shape=jax.ShapeDtypeStruct((PIECE, columns), jnp.bfloat16),
        in_specs=[smem] + [vmem] * 4,
        out_specs=vmem,
        scratch_shapes=[pltpu.VMEM((PIECE, columns), jnp.bfloat16)],
        name="prep",
    )(
        block_dims,
        amplitudes,
        moved,
        jnp.asarray(compact_tables(width)),
        jnp.asarray(compact_tables(least)),
    )


def cut_rows(ints, keep):
    out_columns = ints.shape[-1]
    rows = ints.reshape(4, -1, 4, BS, out_columns)[:, :, :, :keep]
    return rows.transpose(1, 0, 2, 3, 4).reshape(-1, out_columns)


def pad_rows(rows, count):
    return jnp.pad(rows, ((0, count - rows.shape[0]), (0, 0)))


def own_rows(ladder_ints, width, least, columns, core):
    out_columns = ladder_ints.shape[1]

    def of_first():
        groups = ladder_ints.reshape(4, 4, 4 * BS, out_columns)
        return pad_rows(cut_rows(groups[:, :3], width), columns)

    def of_second():
        return pad_rows(cut_rows(ladder_ints, least), columns)

    return lax.cond(core == 0, of_first, of_second)


def distance_of(slot, core):
    swapped = (slot & 1) * 2 + (slot >> 1)
    return jnp.where(core == 0, slot, swapped)


def chip_of(n, core, blk_index):
    near = (n >= 4) & (n < 12)
    z_step = jnp.where(near, (n & 1) * 2 + 1, jnp.where(n < 4, 0, 2))
    slot = jnp.where(near, (n - 4) >> 1, n & 3)
    z = (blk_index // 4 - z_step) & 3
    return z * 4 + ((blk_index & 3) ^ distance_of(slot, core))


VMEM = pl.BlockSpec(memory_space=pltpu.VMEM)
SMEM = pl.BlockSpec(memory_space=pltpu.SMEM)
ROOM = pltpu.CompilerParams(vmem_limit_bytes=48 * 1024 * 1024)
SHORT = pl.CostEstimate(flops=1024, bytes_accessed=1024, transcendentals=0)
STAGES = (10, 6)


def slots_kernel(part_0, part_1, part_2, part_3, here, there):
    core, blk_index = lax.axis_index("slab"), lax.axis_index("blk")
    occupied = part_0.shape[1]
    slot = lax.broadcasted_iota(jnp.int32, (128, 1), 0)
    at = lax.broadcasted_iota(jnp.int32, (128, occupied), 1)
    for order, out in ((core, here), (1 - core, there)):
        chip = chip_of(slot >> 3, order, blk_index)
        k = 15 * (chip >> 1) + 7 * (chip & 1) + (slot & 7)
        pick = jnp.where(at == k, 1.0, 0.0).astype(jnp.bfloat16)
        for step, part in enumerate((part_0, part_1, part_2, part_3)):
            first = (blk_index // 4 - step & 3) * 4
            part = jnp.concatenate([part[c] for c in range(4)], 1)
            rows = jnp.dot(pick, part, preferred_element_type=jnp.float32).astype(jnp.bfloat16)
            for c in range(4):
                lo = 0
                for stage in STAGES:
                    each = 8 * stage
                    to = pl.multiple_of(GROUP * lo + (first + c) * each, 16)
                    out[pl.ds(to, each), :] = rows[lo : lo + each, 128 * c : 128 * c + 128]
                    lo += each


def slots_of_pieces(parts):
    shape = jax.ShapeDtypeStruct((GROUP * 128, 128), jnp.bfloat16)
    return pl.pallas_call(
        slots_kernel,
        out_shape=[shape, shape],
        in_specs=[VMEM] * 4,
        out_specs=[VMEM] * 2,
        compiler_params=ROOM,
        cost_estimate=SHORT,
        name="slots",
    )(*parts)


def products(pieces, rows_w, total):
    depth = rows_w.shape[0]
    step = max(n for n in range(128, 513, 128) if depth % n == 0)
    total[...] = jnp.zeros_like(total)

    def body(n, carry):
        at = pl.ds(pl.multiple_of(n * step, 128), step)
        left = [piece[:, :, at].reshape(-1, step) for piece in pieces]
        total[...] += jnp.dot(
            jnp.concatenate(left, 0), rows_w[at, :], preferred_element_type=jnp.float32
        )
        return carry

    lax.fori_loop(0, depth // step, body, 0)


def ladder_part_kernel(*refs):
    products(refs[:-2], refs[-2], refs[-1])


def ladder_part(pieces, rows_w):
    count = sum(piece.shape[0] for piece in pieces)
    shape = (count * PIECE, rows_w.shape[1])
    return pl.pallas_call(
        ladder_part_kernel,
        out_shape=jax.ShapeDtypeStruct(shape, jnp.float32),
        in_specs=[VMEM] * (len(pieces) + 1),
        out_specs=VMEM,
        compiler_params=ROOM,
        cost_estimate=SHORT,
        name="ladder_part",
    )(*pieces, rows_w)


def ladder_late_kernel(*refs):
    pieces = refs[:-5]
    rows_w, early, mine, other, total = refs[-5:]
    core, blk_index = lax.axis_index("slab"), lax.axis_index("blk")
    products(pieces, rows_w, total)

    def place(first, sums):
        def body(n, carry):
            chip = chip_of(first + n, core, blk_index)
            value = sums[pl.ds(pl.multiple_of(n * PIECE, PIECE), PIECE), :]

            @pl.when(chip // 8 == core)
            def _():
                mine[chip & 7] = value

            @pl.when(chip // 8 != core)
            def _():
                other[chip & 7] = value

            return carry

        lax.fori_loop(0, sums.shape[0] // PIECE, body, 0)

    place(0, early)
    place(STAGES[0], total)


def ladder_late(pieces, rows_w, early):
    out_columns = rows_w.shape[1]
    half = jax.ShapeDtypeStruct((8, PIECE, out_columns), jnp.float32)
    return pl.pallas_call(
        ladder_late_kernel,
        out_shape=[half, half],
        in_specs=[VMEM] * (len(pieces) + 2),
        out_specs=[VMEM, VMEM],
        scratch_shapes=[pltpu.VMEM((STAGES[1] * PIECE, out_columns), jnp.float32)],
        compiler_params=ROOM,
        cost_estimate=SHORT,
        name="ladder_late",
    )(*pieces, rows_w, early)


def ladder_end_kernel(dims, mine, other, out, rows):
    out_columns = out.shape[1]
    column = lax.axis_index("blk") * out_columns
    column = column + lax.broadcasted_iota(jnp.int32, (1, out_columns), 1)
    block, c, d = column >> 12, column >> 6 & 63, column & 63
    size_first = jnp.where(block == 0, dims[0, 0], dims[1, 0])
    size_second = jnp.where(block == 0, dims[0, 1], dims[1, 1])
    keep = (c < size_first) & (d < size_second)

    def body(pair, carry):
        even = mine[2 * pair] + other[2 * pair]
        odd = mine[2 * pair + 1] + other[2 * pair + 1]
        both = jnp.concatenate([even[:56], even[56:] + odd[:8], odd[8:]], 0)
        rows[pl.ds(pl.multiple_of(pair * 120, 8), 120), :] = jnp.where(keep, both, 0.0)
        return carry

    lax.fori_loop(0, 4, body, 0)
    out[...] = rows[...].astype(jnp.bfloat16)


def ladder_end(block_dims, mine, other):
    shape = (480, mine.shape[2])
    return pl.pallas_call(
        ladder_end_kernel,
        out_shape=jax.ShapeDtypeStruct(shape, jnp.bfloat16),
        in_specs=[SMEM] + [VMEM] * 2,
        out_specs=VMEM,
        scratch_shapes=[pltpu.VMEM(shape, jnp.float32)],
        compiler_params=ROOM,
        cost_estimate=SHORT,
        name="ladder_end",
    )(block_dims, mine, other)


def turn(pieces, group_width, start, spread, turned):
    wide = GROUP * group_width
    count = sum(piece.shape[0] for piece in pieces)
    rows, each = count * PIECE, 8 * count
    n = 0
    for piece in pieces:

        def body(i, carry, piece=piece, n=n):
            part = piece[i, :, pl.ds(start, wide)].astype(jnp.float32)
            for b in range(wide // 128):
                at = pl.multiple_of((b * count + n + i) * PIECE, PIECE)
                spread[pl.ds(at, PIECE), :] = part[:, 128 * b : 128 * b + 128]
            return carry

        lax.fori_loop(0, piece.shape[0], body, 0)
        n += piece.shape[0]
    spread[wide // 128 * rows : wide // 128 * rows + rows, :] = jnp.zeros((rows, 128), jnp.float32)

    def columns(pair, carry):
        for c in range(GROUP):
            lo = c * group_width
            base = lo // 128
            blocks = [base] if lo % 128 + BS <= 128 else [base, base + 1]
            halves = []
            for odd in range(2):
                window = [
                    spread[pl.ds(b * rows + 2 * pair + odd, each, stride=8), :] for b in blocks
                ]
                window = jnp.concatenate(window, 1)
                halves.append(window[:, lo % 128 : lo % 128 + BS])
            at = pl.ds(pl.multiple_of(pair * 128, 128), 128)
            turned[c * each : (c + 1) * each, at] = jnp.concatenate(halves, 1).astype(turned.dtype)
        return carry

    lax.fori_loop(0, 4, columns, 0)


def first_part(core, plane):
    return (core == 0) == (plane < 3)


def group_starts(width, least, core, plane):
    first = jnp.where(core == 0, plane * (GROUP * width), 4 * GROUP * least)
    own = plane * (GROUP * least)
    return pl.multiple_of(first, 128), pl.multiple_of(own, 128)


def cycle_early_kernel(width, least, *refs):
    pieces, (first, own, spread) = refs[:-3], refs[-3:]
    core, plane = lax.axis_index("slab"), lax.axis_index("blk") & 3
    first_start, own_start = group_starts(width, least, core, plane)

    @pl.when(first_part(core, plane))
    def _():
        turn(pieces, width, first_start, spread, first)

    @pl.when(core == 1)
    def _():
        turn(pieces, least, own_start, spread, own)


def cycle_early(width, least, pieces):
    count = sum(p.shape[0] for p in pieces)
    shape = jax.ShapeDtypeStruct((GROUP * 8 * count, 8 * BS), jnp.bfloat16)
    blocks = GROUP * max(width, least) // 128 + 1
    return pl.pallas_call(
        functools.partial(cycle_early_kernel, width, least),
        out_shape=[shape, shape],
        in_specs=[VMEM] * len(pieces),
        out_specs=[VMEM, VMEM],
        scratch_shapes=[pltpu.VMEM((blocks * count * PIECE, 128), jnp.float32)],
        compiler_params=ROOM,
        cost_estimate=SHORT,
        name="cycle_early",
    )(*pieces)


def cycle_late_kernel(width, least, row, *refs):
    pieces, refs = refs[:-8], refs[-8:]
    before_first, before_own, slots_first, slots_own, first, own, spread, turned = refs
    core, plane = lax.axis_index("slab"), lax.axis_index("blk") & 3
    first_start, own_start = group_starts(width, least, core, plane)

    def add(slots, row, right):
        return lax.dot_general(
            slots[row : row + right.shape[0], :],
            right[...],
            (((0,), (0,)), ((), ())),
            preferred_element_type=jnp.float32,
        )

    def total(group_width, start, slots, before, out):
        turn(pieces, group_width, start, spread, turned)
        value = add(slots, 0, before) + add(slots, row, turned)
        for n in range(4):
            to = pl.multiple_of((plane ^ n) * 32, 32)
            out[pl.ds(to, 32), :] = value[32 * n : 32 * n + 32]

    first[...] = jnp.zeros_like(first)
    own[...] = jnp.zeros_like(own)

    @pl.when(first_part(core, plane))
    def _():
        total(width, first_start, slots_first, before_first, first)

    @pl.when(core == 1)
    def _():
        total(least, own_start, slots_own, before_own, own)

    @pl.when(core == 0)
    def _():
        own[...] = first[...]


def cycle_late(width, least, pieces, turned, slots_first, slots_own):
    count = STAGES[1]
    shape = jax.ShapeDtypeStruct((128, 8 * BS), jnp.float32)
    blocks = GROUP * max(width, least) // 128 + 1
    row = GROUP * 8 * STAGES[0]
    return pl.pallas_call(
        functools.partial(cycle_late_kernel, width, least, row),
        out_shape=[shape, shape],
        in_specs=[VMEM] * (4 + len(pieces)),
        out_specs=[VMEM, VMEM],
        scratch_shapes=[
            pltpu.VMEM((blocks * count * PIECE, 128), jnp.float32),
            pltpu.VMEM((GROUP * 8 * count, 8 * BS), jnp.bfloat16),
        ],
        compiler_params=ROOM,
        cost_estimate=SHORT,
        name="cycle_late",
    )(*pieces, *turned, slots_first, slots_own)


def cycle_end_kernel(dims, part_0, part_1, part_2, part_3, out):
    core, blk_index = lax.axis_index("slab"), lax.axis_index("blk")
    rows, columns = part_0.shape
    a = blk_index * rows + lax.broadcasted_iota(jnp.int32, (rows, columns), 0) & (BS - 1)
    d = lax.broadcasted_iota(jnp.int32, (rows, columns), 1) & (BS - 1)
    keep = (a < dims[core, 0]) & (d < dims[core, 1])
    total = part_0[...] + part_1[...] + part_2[...] + part_3[...]
    out[0] = jnp.where(keep, total, 0.0).astype(jnp.bfloat16)


def cycle_end(block_dims, parts):
    return pl.pallas_call(
        cycle_end_kernel,
        out_shape=jax.ShapeDtypeStruct((1,) + parts[0].shape, jnp.bfloat16),
        in_specs=[SMEM] + [VMEM] * 4,
        out_specs=VMEM,
        compiler_params=ROOM,
        cost_estimate=SHORT,
        name="cycle_end",
    )(block_dims, *parts)


def together(*values):
    return lax.optimization_barrier(values)


def after(value, *others):
    return together(value, *others)[0]


def compacted(width, least, amplitudes, ladder_ints, cycle_ints, block_dims, moved):
    core = lax.axis_index("slab")
    blk_index = lax.axis_index("blk")
    plane, z = blk_index % 4, blk_index // 4
    wide_columns, narrow_columns = GROUP * width, GROUP * least
    columns = max(3 * wide_columns, wide_columns + 4 * narrow_columns)

    own = prep(width, least, columns, block_dims, amplitudes, moved)[None]
    near = [send(own, up(step)) for step in (1, 3)]
    plane_1 = send(own, first_axis)
    plane_2 = send(own, second_axis)
    plane_12 = send(plane_1, second_axis)
    ints, shares = together(ladder_ints, cycle_ints[0], own)[:2]
    moved_ints = ints.reshape(4, 4, 4 * BS, -1)[:, 3].reshape(GROUP * BS, -1)
    shares = [lax.dynamic_slice_in_dim(shares, (z + step) % 4 * 128, 128, 2) for step in range(4)]
    rows_w = own_rows(ints, width, least, columns, core)
    near, far, moved_ints, rows_w, *shares = together(
        jnp.concatenate(near), own, moved_ints, rows_w, *shares, plane_1, plane_2, plane_12
    )[:8]
    far = send(far, up(2))
    near_1 = send(near, first_axis)
    near_2 = send(near, second_axis)
    moved_ints = to_other_core(moved_ints, (0,))
    far, near_1, near_2, rows_w, moved_ints, *shares = together(
        far, near_1, near_2, rows_w, moved_ints, *shares
    )
    cut = 4 * narrow_columns
    moved_rows = pad_rows(cut_rows(moved_ints, width), columns - cut)
    rows_w = lax.dynamic_update_slice(
        rows_w, jnp.where(core == 0, rows_w[cut:], moved_rows), (cut, 0)
    )
    far_1 = send(far, first_axis)
    far_2 = send(far, second_axis)
    near_12 = send(near_1, second_axis)
    shares[3] = send(shares[3], up(3))
    shares[2] = send(shares[2], up(2))
    shares[1] = send(after(shares[1], shares[3]), up(1))
    early = [own, plane_1, plane_2, plane_12, near, near_1, near_2]
    sums = ladder_part(early, rows_w)
    turned = cycle_early(width, least, early)
    far_1, far_2, near_12, sums, turned, *shares = together(
        far_1, far_2, near_12, sums, turned, *shares
    )
    far_12 = send(far_1, second_axis)
    slots, there = slots_of_pieces(shares)
    there = to_other_core(there, (0,))
    near_12, far_12, slots, there = together(near_12, far_12, slots, there)
    slots_first = jnp.where(core == 0, slots, there)
    late = [near_12, far, far_1, far_2, far_12]
    terms = cycle_late(width, least, late, turned, slots_first, slots)
    pairs = [(2 * chip + 1, 2 * chip) for chip in (3, 7, 11, 15)]
    last_group = lax.ppermute(terms[0], AXES, pairs)
    mine, other = ladder_late(late, rows_w, after(sums, terms[1]))
    other = to_other_core(other, (0, 1))
    term = (terms[1] + last_group).reshape(4, 32, 8 * BS)
    parts = [send(term[n], target) for n, target in ((1, along_x), (2, along_y), (3, across))]
    ladder_res = ladder_end(block_dims, mine, other)
    cycle_res = cycle_end(block_dims, [after(term[0], ladder_res)] + parts)
    return (ladder_res, cycle_res)


WIDTHS = (48, 56, 64)


def local(amplitudes, ladder_ints, cycle_ints, block_dims):
    moved = to_other_core(amplitudes, (0,))
    fits = [block_dims[0, 1] > width for width in WIDTHS[:-1]]
    choice = sum(fit.astype(jnp.int32) for fit in fits)
    choice = jnp.where(block_dims[1, 1] <= LEAST, choice, len(WIDTHS))
    branches = [functools.partial(compacted, width, LEAST) for width in WIDTHS]
    branches.append(functools.partial(compacted, BS, BS))
    return lax.switch(
        choice, branches, amplitudes, ladder_ints, cycle_ints, block_dims, moved
    )


def solution(mesh):
    in_specs = (P("blk", "slab"), P("slab", "blk"), P("slab", "blk", None, None), P())
    out_specs = (P("slab", "blk"), P("slab", "blk", None))
    body = local if dict(mesh.shape) == {"blk": 16, "slab": 2} else plain
    return jax.shard_map(body, mesh=mesh, in_specs=in_specs, out_specs=out_specs, check_vma=False)
```

```python
import functools

import jax
import jax.numpy as jnp
import numpy as np
from jax import lax
from jax.experimental import pallas as pl
from jax.experimental.pallas import tpu as pltpu
from jax.sharding import PartitionSpec as P

BS = 64
LEAST = 24
GROUP = 16
PIECE = 64
AXES = ("blk", "slab")
LAST_CHIPS = (3, 7, 11, 15)


def block_sizes(block_dims, owner):
    blocks_count = block_dims.shape[0]
    select = owner[:, None] == lax.iota(jnp.int32, blocks_count)[None, :]
    size_first = jnp.sum(jnp.where(select, block_dims[None, :, 0], 0), 1)
    size_second = jnp.sum(jnp.where(select, block_dims[None, :, 1], 0), 1)
    return (size_first, size_second)


def column_valid(block_dims, first_column, column_count):
    column = first_column + lax.iota(jnp.int32, column_count)
    owner = column // (BS * BS)
    size_first, size_second = block_sizes(block_dims, owner)
    return (column // BS % BS < size_first) & (column % BS < size_second)


def cycle_allowed(block_dims, slab_index, blk_index, local_rows, columns):
    own_block = jnp.full((1,), slab_index, jnp.int32)
    size_first, size_second = block_sizes(block_dims, own_block)
    row_virtual = (blk_index * local_rows + lax.iota(jnp.int32, local_rows)) % BS
    column_virtual = lax.iota(jnp.int32, columns) % BS
    return (row_virtual[:, None] < size_first[0]) & (column_virtual[None, :] < size_second[0])


def plain(amplitudes, ladder_ints, cycle_ints, block_dims):
    slab_index = lax.axis_index("slab")
    blk_index = lax.axis_index("blk")
    block_width = amplitudes.shape[1]
    valid = column_valid(block_dims, slab_index * block_width, block_width)
    masked = jnp.where(valid[None, :], amplitudes, jnp.zeros((), amplitudes.dtype))
    gathered = lax.all_gather(masked, "blk", axis=0, tiled=True)
    pair_rows = gathered.shape[0]
    ladder_sum = lax.psum_scatter(
        jnp.dot(gathered, ladder_ints, preferred_element_type=jnp.float32),
        "slab",
        scatter_dimension=0,
        tiled=True,
    )
    out_columns = ladder_ints.shape[1]
    out_valid = column_valid(block_dims, blk_index * out_columns, out_columns)
    ladder_res = jnp.where(out_valid[None, :], ladder_sum, 0.0).astype(jnp.bfloat16)
    occupied = cycle_ints.shape[2]
    j_window = pair_rows // occupied
    columns = lax.all_to_all(masked, "blk", split_axis=1, concat_axis=0, tiled=True)
    c_part = cycle_ints.shape[1]
    amp_part = columns.reshape(occupied, j_window, c_part, BS)
    cycle_term = jnp.einsum(
        "cke,kjcd->ejd", cycle_ints[0], amp_part, preferred_element_type=jnp.float32
    )
    cycle_term = cycle_term.reshape(cycle_term.shape[0], j_window * BS)
    cycle_sum = lax.psum_scatter(cycle_term, "blk", scatter_dimension=0, tiled=True)
    allowed = cycle_allowed(block_dims, slab_index, blk_index, cycle_sum.shape[0], j_window * BS)
    cycle_res = jnp.where(allowed, cycle_sum, 0.0).astype(jnp.bfloat16)[None]
    return (ladder_res, cycle_res)


def send(value, target, cores=(0, 1)):
    pairs = []
    for chip in range(16):
        for core in cores:
            x, y, z = target(chip & 1, chip >> 1 & 1, chip >> 2, core)
            pairs.append((2 * chip + core, 2 * (4 * (z % 4) + 2 * y + x) + core))
    return lax.ppermute(value, AXES, pairs)


def along_x(x, y, z, core):
    return (1 - x, y, z)


def along_y(x, y, z, core):
    return (x, 1 - y, z)


def across(x, y, z, core):
    return (1 - x, 1 - y, z)


def first_axis(x, y, z, core):
    return along_x(x, y, z, core) if core == 0 else along_y(x, y, z, core)


def second_axis(x, y, z, core):
    return along_y(x, y, z, core) if core == 0 else along_x(x, y, z, core)


def up(step):
    return lambda x, y, z, core: (x, y, z + step)


def to_other_core(value, cores):
    return lax.ppermute(value, "slab", [(core, 1 - core) for core in cores])


def compact_tables(width):
    column = np.arange(GROUP * width)
    c, d = column // width, column % width
    return np.stack([c * BS + d, c // 4 * GROUP + c % 4, d] + [c * 0] * 5).astype(np.int32)


def prep_kernel(width, least, dims, amp, moved, wide, narrow, out, rows):
    def tiles(table, group_width):
        result = []
        for lo in range(0, GROUP * group_width, 128):
            start = lo // group_width // 2 * 128
            stop = -(-((lo + 127) // group_width + 1) // 2) * 128
            source = table[0:1, lo : lo + 128] - start
            at = lax.broadcasted_iota(jnp.int32, (stop - start, 128), 0)
            pick = jnp.where(at == source, 1.0, 0.0).astype(jnp.bfloat16)
            result.append((lo, start, stop, pick))
        return result

    def compact(source, group, table, picks, block, to):
        def part(at):
            column = at // (4 * BS) * (GROUP * BS) + group * (4 * BS) + at % (4 * BS)
            return source[:, column : column + 128]

        for lo, start, stop, pick in picks:
            window = jnp.concatenate([part(at) for at in range(start, stop, 128)], 1)
            value = jnp.dot(window, pick, preferred_element_type=jnp.float32)
            c, d = table[1:2, lo : lo + 128] + 4 * group, table[2:3, lo : lo + 128]
            keep = (c < dims[block, 0]) & (d < dims[block, 1])
            rows[0:60, to + lo : to + lo + 128] = jnp.where(keep, value, 0.0).astype(jnp.bfloat16)

    core, shift = lax.axis_index("slab"), lax.axis_index("blk") % 2 * 4
    wide_columns, narrow_columns = GROUP * width, GROUP * least
    rows[...] = jnp.zeros_like(rows)

    @pl.when(core == 0)
    def _():
        picks = tiles(wide, width)
        for g in range(3):
            compact(amp, g, wide, picks, 0, g * wide_columns)

    @pl.when(core == 1)
    def _():
        picks = tiles(narrow, least)
        for g in range(4):
            compact(amp, g, narrow, picks, 1, g * narrow_columns)
        compact(moved, 3, wide, tiles(wide, width), 0, 4 * narrow_columns)

    shape = (PIECE, PIECE)
    down = lax.broadcasted_iota(jnp.int32, shape, 0) - lax.broadcasted_iota(jnp.int32, shape, 1)
    down = jnp.where(down == shift, 1.0, 0.0).astype(jnp.bfloat16)
    out[...] = jnp.dot(down, rows[...], preferred_element_type=jnp.float32).astype(jnp.bfloat16)


def prep(width, least, columns, block_dims, amplitudes, moved):
    smem = pl.BlockSpec(memory_space=pltpu.SMEM)
    vmem = pl.BlockSpec(memory_space=pltpu.VMEM)
    return pl.pallas_call(
        functools.partial(prep_kernel, width, least),
        out_shape=jax.ShapeDtypeStruct((PIECE, columns), jnp.bfloat16),
        in_specs=[smem] + [vmem] * 4,
        out_specs=vmem,
        scratch_shapes=[pltpu.VMEM((PIECE, columns), jnp.bfloat16)],
        name="prep",
    )(
        block_dims,
        amplitudes,
        moved,
        jnp.asarray(compact_tables(width)),
        jnp.asarray(compact_tables(least)),
    )


def cut_rows(ints, keep):
    out_columns = ints.shape[-1]
    rows = ints.reshape(4, -1, 4, BS, out_columns)[:, :, :, :keep]
    return rows.transpose(1, 0, 2, 3, 4).reshape(-1, out_columns)


def pad_rows(rows, count):
    return jnp.pad(rows, ((0, count - rows.shape[0]), (0, 0)))


def own_rows(ladder_ints, width, least, columns, core):
    out_columns = ladder_ints.shape[1]

    def of_first():
        groups = ladder_ints.reshape(4, 4, 4 * BS, out_columns)
        return pad_rows(cut_rows(groups[:, :3], width), columns)

    def of_second():
        return pad_rows(cut_rows(ladder_ints, least), columns)

    return lax.cond(core == 0, of_first, of_second)


def distance_of(slot, core):
    swapped = (slot & 1) * 2 + (slot >> 1)
    return jnp.where(core == 0, slot, swapped)


def chip_of(n, core, blk_index):
    near = (n >= 4) & (n < 12)
    z_step = jnp.where(near, (n & 1) * 2 + 1, jnp.where(n < 4, 0, 2))
    slot = jnp.where(near, (n - 4) >> 1, n & 3)
    z = (blk_index // 4 - z_step) & 3
    return z * 4 + ((blk_index & 3) ^ distance_of(slot, core))


VMEM = pl.BlockSpec(memory_space=pltpu.VMEM)
SMEM = pl.BlockSpec(memory_space=pltpu.SMEM)
ROOM = pltpu.CompilerParams(vmem_limit_bytes=48 * 1024 * 1024)
SHORT = pl.CostEstimate(flops=1024, bytes_accessed=1024, transcendentals=0)
STAGES = (10, 6)


def slots_kernel(part_0, part_1, part_2, part_3, here, there):
    core, blk_index = lax.axis_index("slab"), lax.axis_index("blk")
    occupied = part_0.shape[1]
    slot = lax.broadcasted_iota(jnp.int32, (128, 1), 0)
    at = lax.broadcasted_iota(jnp.int32, (128, occupied), 1)
    for order, out in ((core, here), (1 - core, there)):
        chip = chip_of(slot >> 3, order, blk_index)
        k = 15 * (chip >> 1) + 7 * (chip & 1) + (slot & 7)
        pick = jnp.where(at == k, 1.0, 0.0).astype(jnp.bfloat16)
        for step, part in enumerate((part_0, part_1, part_2, part_3)):
            first = (blk_index // 4 - step & 3) * 4
            part = jnp.concatenate([part[c] for c in range(4)], 1)
            rows = jnp.dot(pick, part, preferred_element_type=jnp.float32).astype(jnp.bfloat16)
            for c in range(4):
                lo = 0
                for stage in STAGES:
                    each = 8 * stage
                    to = pl.multiple_of(GROUP * lo + (first + c) * each, 16)
                    out[pl.ds(to, each), :] = rows[lo : lo + each, 128 * c : 128 * c + 128]
                    lo += each


def slots_of_pieces(parts):
    shape = jax.ShapeDtypeStruct((GROUP * 128, 128), jnp.bfloat16)
    return pl.pallas_call(
        slots_kernel,
        out_shape=[shape, shape],
        in_specs=[VMEM] * 4,
        out_specs=[VMEM] * 2,
        compiler_params=ROOM,
        cost_estimate=SHORT,
        name="slots",
    )(*parts)


def products(pieces, rows_w, total):
    depth = rows_w.shape[0]
    step = max(n for n in range(128, 513, 128) if depth % n == 0)
    total[...] = jnp.zeros_like(total)

    def body(n, carry):
        at = pl.ds(pl.multiple_of(n * step, 128), step)
        left = [piece[:, :, at].reshape(-1, step) for piece in pieces]
        total[...] += jnp.dot(
            jnp.concatenate(left, 0), rows_w[at, :], preferred_element_type=jnp.float32
        )
        return carry

    lax.fori_loop(0, depth // step, body, 0)


def ladder_kernel(first, pieces, rows_w, mine, other, total):
    core, blk_index = lax.axis_index("slab"), lax.axis_index("blk")
    products(pieces, rows_w, total)

    def body(n, carry):
        chip = chip_of(first + n, core, blk_index)
        value = total[pl.ds(pl.multiple_of(n * PIECE, PIECE), PIECE), :]

        @pl.when(chip // 8 == core)
        def _():
            mine[chip & 7] = value

        @pl.when(chip // 8 != core)
        def _():
            other[chip & 7] = value

        return carry

    lax.fori_loop(0, total.shape[0] // PIECE, body, 0)


def ladder_early_kernel(*refs):
    ladder_kernel(0, refs[:-4], *refs[-4:])


def ladder_late_kernel(*refs):
    ladder_kernel(STAGES[0], refs[:-6], refs[-6], *refs[-3:])


def ladder(stage, pieces, rows_w, before=()):
    out_columns = rows_w.shape[1]
    half = jax.ShapeDtypeStruct((8, PIECE, out_columns), jnp.float32)
    given = len(pieces) + 1
    return pl.pallas_call(
        ladder_late_kernel if stage else ladder_early_kernel,
        out_shape=[half, half],
        in_specs=[VMEM] * (given + len(before)),
        out_specs=[VMEM, VMEM],
        scratch_shapes=[pltpu.VMEM((STAGES[stage] * PIECE, out_columns), jnp.float32)],
        input_output_aliases={given + n: n for n in range(len(before))},
        compiler_params=ROOM,
        cost_estimate=SHORT,
        name="ladder_late" if stage else "ladder_early",
    )(*pieces, rows_w, *before)


def ladder_end_kernel(dims, mine, other, out, rows):
    out_columns = out.shape[1]
    column = lax.axis_index("blk") * out_columns
    column = column + lax.broadcasted_iota(jnp.int32, (1, out_columns), 1)
    block, c, d = column >> 12, column >> 6 & 63, column & 63
    size_first = jnp.where(block == 0, dims[0, 0], dims[1, 0])
    size_second = jnp.where(block == 0, dims[0, 1], dims[1, 1])
    keep = (c < size_first) & (d < size_second)

    def body(pair, carry):
        even = mine[2 * pair] + other[2 * pair]
        odd = mine[2 * pair + 1] + other[2 * pair + 1]
        both = jnp.concatenate([even[:56], even[56:] + odd[:8], odd[8:]], 0)
        rows[pl.ds(pl.multiple_of(pair * 120, 8), 120), :] = jnp.where(keep, both, 0.0)
        return carry

    lax.fori_loop(0, 4, body, 0)
    out[...] = rows[...].astype(jnp.bfloat16)


def ladder_end(block_dims, mine, other):
    shape = (480, mine.shape[2])
    return pl.pallas_call(
        ladder_end_kernel,
        out_shape=jax.ShapeDtypeStruct(shape, jnp.bfloat16),
        in_specs=[SMEM] + [VMEM] * 2,
        out_specs=VMEM,
        scratch_shapes=[pltpu.VMEM(shape, jnp.float32)],
        compiler_params=ROOM,
        cost_estimate=SHORT,
        name="ladder_end",
    )(block_dims, mine, other)


def turn(pieces, group_width, start, spread, turned):
    wide = GROUP * group_width
    count = sum(piece.shape[0] for piece in pieces)
    rows, each = count * PIECE, 8 * count
    n = 0
    for piece in pieces:

        def body(i, carry, piece=piece, n=n):
            part = piece[i, :, pl.ds(start, wide)].astype(jnp.float32)
            for b in range(wide // 128):
                at = pl.multiple_of((b * count + n + i) * PIECE, PIECE)
                spread[pl.ds(at, PIECE), :] = part[:, 128 * b : 128 * b + 128]
            return carry

        lax.fori_loop(0, piece.shape[0], body, 0)
        n += piece.shape[0]
    spread[wide // 128 * rows : wide // 128 * rows + rows, :] = jnp.zeros((rows, 128), jnp.float32)

    def columns(pair, carry):
        for c in range(GROUP):
            lo = c * group_width
            base = lo // 128
            blocks = [base] if lo % 128 + BS <= 128 else [base, base + 1]
            halves = []
            for odd in range(2):
                window = [
                    spread[pl.ds(b * rows + 2 * pair + odd, each, stride=8), :] for b in blocks
                ]
                window = jnp.concatenate(window, 1)
                halves.append(window[:, lo % 128 : lo % 128 + BS])
            at = pl.ds(pl.multiple_of(pair * 128, 128), 128)
            turned[c * each : (c + 1) * each, at] = jnp.concatenate(halves, 1).astype(turned.dtype)
        return carry

    lax.fori_loop(0, 4, columns, 0)


def first_part(core, plane):
    return (core == 0) == (plane < 3)


def group_starts(width, least, core, plane):
    first = jnp.where(core == 0, plane * (GROUP * width), 4 * GROUP * least)
    own = plane * (GROUP * least)
    return pl.multiple_of(first, 128), pl.multiple_of(own, 128)


def cycle_early_kernel(width, least, *refs):
    pieces, (first, own, spread) = refs[:-3], refs[-3:]
    core, plane = lax.axis_index("slab"), lax.axis_index("blk") & 3
    first_start, own_start = group_starts(width, least, core, plane)

    @pl.when(first_part(core, plane))
    def _():
        turn(pieces, width, first_start, spread, first)

    @pl.when(core == 1)
    def _():
        turn(pieces, least, own_start, spread, own)


def cycle_early(width, least, pieces):
    count = sum(p.shape[0] for p in pieces)
    shape = jax.ShapeDtypeStruct((GROUP * 8 * count, 8 * BS), jnp.bfloat16)
    blocks = GROUP * max(width, least) // 128 + 1
    return pl.pallas_call(
        functools.partial(cycle_early_kernel, width, least),
        out_shape=[shape, shape],
        in_specs=[VMEM] * len(pieces),
        out_specs=[VMEM, VMEM],
        scratch_shapes=[pltpu.VMEM((blocks * count * PIECE, 128), jnp.float32)],
        compiler_params=ROOM,
        cost_estimate=SHORT,
        name="cycle_early",
    )(*pieces)


def cycle_late_kernel(width, least, row, *refs):
    pieces, refs = refs[:-8], refs[-8:]
    before_first, before_own, slots_first, slots_own, first, own, spread, turned = refs
    core, plane = lax.axis_index("slab"), lax.axis_index("blk") & 3
    first_start, own_start = group_starts(width, least, core, plane)

    def add(slots, row, right):
        return lax.dot_general(
            slots[row : row + right.shape[0], :],
            right[...],
            (((0,), (0,)), ((), ())),
            preferred_element_type=jnp.float32,
        )

    def total(group_width, start, slots, before, out):
        turn(pieces, group_width, start, spread, turned)
        value = add(slots, 0, before) + add(slots, row, turned)
        for n in range(4):
            to = pl.multiple_of((plane ^ n) * 32, 32)
            out[pl.ds(to, 32), :] = value[32 * n : 32 * n + 32]

    first[...] = jnp.zeros_like(first)
    own[...] = jnp.zeros_like(own)

    @pl.when(first_part(core, plane))
    def _():
        total(width, first_start, slots_first, before_first, first)

    @pl.when(core == 1)
    def _():
        total(least, own_start, slots_own, before_own, own)

    @pl.when(core == 0)
    def _():
        own[...] = first[...]


def cycle_late(width, least, pieces, turned, slots_first, slots_own):
    count = STAGES[1]
    shape = jax.ShapeDtypeStruct((128, 8 * BS), jnp.float32)
    blocks = GROUP * max(width, least) // 128 + 1
    row = GROUP * 8 * STAGES[0]
    return pl.pallas_call(
        functools.partial(cycle_late_kernel, width, least, row),
        out_shape=[shape, shape],
        in_specs=[VMEM] * (4 + len(pieces)),
        out_specs=[VMEM, VMEM],
        scratch_shapes=[
            pltpu.VMEM((blocks * count * PIECE, 128), jnp.float32),
            pltpu.VMEM((GROUP * 8 * count, 8 * BS), jnp.bfloat16),
        ],
        compiler_params=ROOM,
        cost_estimate=SHORT,
        name="cycle_late",
    )(*pieces, *turned, slots_first, slots_own)


def together(*values):
    return lax.optimization_barrier(values)


def after(value, *others):
    return together(value, *others)[0]


def compacted(width, least, amplitudes, ladder_ints, cycle_ints, block_dims, moved):
    core = lax.axis_index("slab")
    blk_index = lax.axis_index("blk")
    plane, z = blk_index % 4, blk_index // 4
    wide_columns, narrow_columns = GROUP * width, GROUP * least
    columns = max(3 * wide_columns, wide_columns + 4 * narrow_columns)

    own = prep(width, least, columns, block_dims, amplitudes, moved)[None]
    near = [send(own, up(step)) for step in (1, 3)]
    plane_1 = send(own, first_axis)
    plane_2 = send(own, second_axis)
    plane_12 = send(plane_1, second_axis)
    ints, shares = together(ladder_ints, cycle_ints[0], own)[:2]
    moved_ints = ints.reshape(4, 4, 4 * BS, -1)[:, 3].reshape(GROUP * BS, -1)
    shares = [lax.dynamic_slice_in_dim(shares, (z + step) % 4 * 128, 128, 2) for step in range(4)]
    rows_w = own_rows(ints, width, least, columns, core)
    far = send(after(own, *near), up(2))
    dims = after(block_dims, own)
    allowed = cycle_allowed(dims, core, blk_index, 32, 8 * BS).astype(jnp.float32)
    near, moved_ints, rows_w, allowed, *shares = together(
        jnp.concatenate(near), moved_ints, rows_w, allowed, *shares, plane_1, plane_2, plane_12
    )[:8]
    near_1 = send(near, first_axis)
    near_2 = send(near, second_axis)
    moved_ints = to_other_core(moved_ints, (0,))
    *shares, rows_w, moved_ints, near_2, near_1, far = together(
        *shares, rows_w, moved_ints, near_2, near_1, far
    )
    cut = 4 * narrow_columns
    moved_rows = pad_rows(cut_rows(moved_ints, width), columns - cut)
    rows_w = lax.dynamic_update_slice(
        rows_w, jnp.where(core == 0, rows_w[cut:], moved_rows), (cut, 0)
    )
    far_1 = send(far, first_axis)
    far_2 = send(far, second_axis)
    near_12 = send(near_1, second_axis)
    shares[3] = send(shares[3], up(3))
    shares[2] = send(shares[2], up(2))
    shares[1] = send(after(shares[1], shares[3]), up(1))
    early = [own, plane_1, plane_2, plane_12, near, near_1, near_2]
    sums = ladder(0, early, rows_w)
    turned = cycle_early(width, least, early)
    far_1, far_2, near_12, sums, turned, *shares = together(
        far_1, far_2, near_12, sums, turned, *shares
    )
    far_12 = send(far_1, second_axis)
    slots, there = slots_of_pieces(shares)
    there = [
        lax.ppermute(part, AXES, [(2 * chip, 2 * chip + 1) for chip in LAST_CHIPS])
        for part in jnp.split(there, 2)
    ]
    near_12, slots, far_12, *there = together(near_12, slots, far_12, *there)
    slots_first = jnp.where(core == 0, slots, jnp.concatenate(there))
    late = [near_12, far, far_1, far_2, far_12]
    terms = cycle_late(width, least, late, turned, slots_first, slots)
    pairs = [(2 * chip + 1, 2 * chip) for chip in LAST_CHIPS]
    last_group = lax.ppermute(terms[0], AXES, pairs)
    mine, other = ladder(1, late, rows_w, after(sums, terms[1]))
    other = to_other_core(other, (0, 1))
    term = (terms[1] + last_group).reshape(4, 32, 8 * BS)
    parts = [send(term[n], target) for n, target in ((1, along_x), (2, along_y), (3, across))]
    ladder_res = ladder_end(block_dims, mine, other)
    parts = together(term[0], *parts, ladder_res)[:4]
    cycle_sum = parts[0] + parts[1] + parts[2] + parts[3]
    cycle_res = (cycle_sum * allowed).astype(jnp.bfloat16)[None]
    return (ladder_res, cycle_res)


WIDTHS = (48, 56, 64)


def local(amplitudes, ladder_ints, cycle_ints, block_dims):
    moved = to_other_core(amplitudes, (0,))
    fits = [block_dims[0, 1] > width for width in WIDTHS[:-1]]
    choice = sum(fit.astype(jnp.int32) for fit in fits)
    choice = jnp.where(block_dims[1, 1] <= LEAST, choice, len(WIDTHS))
    branches = [functools.partial(compacted, width, LEAST) for width in WIDTHS]
    branches.append(functools.partial(compacted, BS, BS))
    return lax.switch(
        choice, branches, amplitudes, ladder_ints, cycle_ints, block_dims, moved
    )


def solution(mesh):
    in_specs = (P("blk", "slab"), P("slab", "blk"), P("slab", "blk", None, None), P())
    out_specs = (P("slab", "blk"), P("slab", "blk", None))
    body = local if dict(mesh.shape) == {"blk": 16, "slab": 2} else plain
    return jax.shard_map(body, mesh=mesh, in_specs=in_specs, out_specs=out_specs, check_vma=False)
```

```python
import functools

import jax
import jax.numpy as jnp
import numpy as np
from jax import lax
from jax.experimental import pallas as pl
from jax.experimental.pallas import tpu as pltpu
from jax.sharding import PartitionSpec as P

BS = 64
LEAST = 24
GROUP = 16
PIECE = 64
AXES = ("blk", "slab")
LAST_CHIPS = (3, 7, 11, 15)


def block_sizes(block_dims, owner):
    blocks_count = block_dims.shape[0]
    select = owner[:, None] == lax.iota(jnp.int32, blocks_count)[None, :]
    size_first = jnp.sum(jnp.where(select, block_dims[None, :, 0], 0), 1)
    size_second = jnp.sum(jnp.where(select, block_dims[None, :, 1], 0), 1)
    return (size_first, size_second)


def column_valid(block_dims, first_column, column_count):
    column = first_column + lax.iota(jnp.int32, column_count)
    owner = column // (BS * BS)
    size_first, size_second = block_sizes(block_dims, owner)
    return (column // BS % BS < size_first) & (column % BS < size_second)


def cycle_allowed(block_dims, slab_index, blk_index, local_rows, columns):
    own_block = jnp.full((1,), slab_index, jnp.int32)
    size_first, size_second = block_sizes(block_dims, own_block)
    row_virtual = (blk_index * local_rows + lax.iota(jnp.int32, local_rows)) % BS
    column_virtual = lax.iota(jnp.int32, columns) % BS
    return (row_virtual[:, None] < size_first[0]) & (column_virtual[None, :] < size_second[0])


def plain(amplitudes, ladder_ints, cycle_ints, block_dims):
    slab_index = lax.axis_index("slab")
    blk_index = lax.axis_index("blk")
    block_width = amplitudes.shape[1]
    valid = column_valid(block_dims, slab_index * block_width, block_width)
    masked = jnp.where(valid[None, :], amplitudes, jnp.zeros((), amplitudes.dtype))
    gathered = lax.all_gather(masked, "blk", axis=0, tiled=True)
    pair_rows = gathered.shape[0]
    ladder_sum = lax.psum_scatter(
        jnp.dot(gathered, ladder_ints, preferred_element_type=jnp.float32),
        "slab",
        scatter_dimension=0,
        tiled=True,
    )
    out_columns = ladder_ints.shape[1]
    out_valid = column_valid(block_dims, blk_index * out_columns, out_columns)
    ladder_res = jnp.where(out_valid[None, :], ladder_sum, 0.0).astype(jnp.bfloat16)
    occupied = cycle_ints.shape[2]
    j_window = pair_rows // occupied
    columns = lax.all_to_all(masked, "blk", split_axis=1, concat_axis=0, tiled=True)
    c_part = cycle_ints.shape[1]
    amp_part = columns.reshape(occupied, j_window, c_part, BS)
    cycle_term = jnp.einsum(
        "cke,kjcd->ejd", cycle_ints[0], amp_part, preferred_element_type=jnp.float32
    )
    cycle_term = cycle_term.reshape(cycle_term.shape[0], j_window * BS)
    cycle_sum = lax.psum_scatter(cycle_term, "blk", scatter_dimension=0, tiled=True)
    allowed = cycle_allowed(block_dims, slab_index, blk_index, cycle_sum.shape[0], j_window * BS)
    cycle_res = jnp.where(allowed, cycle_sum, 0.0).astype(jnp.bfloat16)[None]
    return (ladder_res, cycle_res)


def send(value, target, cores=(0, 1)):
    pairs = []
    for chip in range(16):
        for core in cores:
            x, y, z = target(chip & 1, chip >> 1 & 1, chip >> 2, core)
            pairs.append((2 * chip + core, 2 * (4 * (z % 4) + 2 * y + x) + core))
    return lax.ppermute(value, AXES, pairs)


def along_x(x, y, z, core):
    return (1 - x, y, z)


def along_y(x, y, z, core):
    return (x, 1 - y, z)


def across(x, y, z, core):
    return (1 - x, 1 - y, z)


def first_axis(x, y, z, core):
    return along_x(x, y, z, core) if core == 0 else along_y(x, y, z, core)


def second_axis(x, y, z, core):
    return along_y(x, y, z, core) if core == 0 else along_x(x, y, z, core)


def up(step):
    return lambda x, y, z, core: (x, y, z + step)


def to_other_core(value, cores):
    return lax.ppermute(value, "slab", [(core, 1 - core) for core in cores])


def compact_tables(width):
    column = np.arange(GROUP * width)
    c, d = column // width, column % width
    return np.stack([c * BS + d, c // 4 * GROUP + c % 4, d] + [c * 0] * 5).astype(np.int32)


def prep_kernel(width, least, dims, amp, moved, wide, narrow, out, rows):
    def tiles(table, group_width):
        result = []
        for lo in range(0, GROUP * group_width, 128):
            start = lo // group_width // 2 * 128
            stop = -(-((lo + 127) // group_width + 1) // 2) * 128
            source = table[0:1, lo : lo + 128] - start
            at = lax.broadcasted_iota(jnp.int32, (stop - start, 128), 0)
            pick = jnp.where(at == source, 1.0, 0.0).astype(jnp.bfloat16)
            result.append((lo, start, stop, pick))
        return result

    def compact(source, group, table, picks, block, to):
        def part(at):
            column = at // (4 * BS) * (GROUP * BS) + group * (4 * BS) + at % (4 * BS)
            return source[:, column : column + 128]

        for lo, start, stop, pick in picks:
            window = jnp.concatenate([part(at) for at in range(start, stop, 128)], 1)
            value = jnp.dot(window, pick, preferred_element_type=jnp.float32)
            c, d = table[1:2, lo : lo + 128] + 4 * group, table[2:3, lo : lo + 128]
            keep = (c < dims[block, 0]) & (d < dims[block, 1])
            rows[0:60, to + lo : to + lo + 128] = jnp.where(keep, value, 0.0).astype(jnp.bfloat16)

    core, shift = lax.axis_index("slab"), lax.axis_index("blk") % 2 * 4
    wide_columns, narrow_columns = GROUP * width, GROUP * least
    rows[...] = jnp.zeros_like(rows)

    @pl.when(core == 0)
    def _():
        picks = tiles(wide, width)
        for g in range(3):
            compact(amp, g, wide, picks, 0, g * wide_columns)

    @pl.when(core == 1)
    def _():
        picks = tiles(narrow, least)
        for g in range(4):
            compact(amp, g, narrow, picks, 1, g * narrow_columns)
        compact(moved, 3, wide, tiles(wide, width), 0, 4 * narrow_columns)

    shape = (PIECE, PIECE)
    down = lax.broadcasted_iota(jnp.int32, shape, 0) - lax.broadcasted_iota(jnp.int32, shape, 1)
    down = jnp.where(down == shift, 1.0, 0.0).astype(jnp.bfloat16)
    out[...] = jnp.dot(down, rows[...], preferred_element_type=jnp.float32).astype(jnp.bfloat16)


def prep(width, least, columns, block_dims, amplitudes, moved):
    smem = pl.BlockSpec(memory_space=pltpu.SMEM)
    vmem = pl.BlockSpec(memory_space=pltpu.VMEM)
    return pl.pallas_call(
        functools.partial(prep_kernel, width, least),
        out_shape=jax.ShapeDtypeStruct((PIECE, columns), jnp.bfloat16),
        in_specs=[smem] + [vmem] * 4,
        out_specs=vmem,
        scratch_shapes=[pltpu.VMEM((PIECE, columns), jnp.bfloat16)],
        name="prep",
    )(
        block_dims,
        amplitudes,
        moved,
        jnp.asarray(compact_tables(width)),
        jnp.asarray(compact_tables(least)),
    )


def cut_rows(ints, keep):
    out_columns = ints.shape[-1]
    rows = ints.reshape(4, -1, 4, BS, out_columns)[:, :, :, :keep]
    return rows.transpose(1, 0, 2, 3, 4).reshape(-1, out_columns)


def pad_rows(rows, count):
    return jnp.pad(rows, ((0, count - rows.shape[0]), (0, 0)))


def own_rows(ladder_ints, width, least, columns, core):
    out_columns = ladder_ints.shape[1]

    def of_first():
        groups = ladder_ints.reshape(4, 4, 4 * BS, out_columns)
        return pad_rows(cut_rows(groups[:, :3], width), columns)

    def of_second():
        return pad_rows(cut_rows(ladder_ints, least), columns)

    return lax.cond(core == 0, of_first, of_second)


def distance_of(slot, core):
    swapped = (slot & 1) * 2 + (slot >> 1)
    return jnp.where(core == 0, slot, swapped)


def chip_of(n, core, blk_index):
    near = (n >= 4) & (n < 12)
    z_step = jnp.where(near, (n & 1) * 2 + 1, jnp.where(n < 4, 0, 2))
    slot = jnp.where(near, (n - 4) >> 1, n & 3)
    z = (blk_index // 4 - z_step) & 3
    return z * 4 + ((blk_index & 3) ^ distance_of(slot, core))


VMEM = pl.BlockSpec(memory_space=pltpu.VMEM)
SMEM = pl.BlockSpec(memory_space=pltpu.SMEM)
ROOM = pltpu.CompilerParams(vmem_limit_bytes=48 * 1024 * 1024)
SHORT = pl.CostEstimate(flops=1024, bytes_accessed=1024, transcendentals=0)
STAGES = (10, 6)


def slots_kernel(part_0, part_1, part_2, part_3, here, there):
    core, blk_index = lax.axis_index("slab"), lax.axis_index("blk")
    occupied = part_0.shape[1]
    slot = lax.broadcasted_iota(jnp.int32, (128, 1), 0)
    at = lax.broadcasted_iota(jnp.int32, (128, occupied), 1)
    for order, out in ((core, here), (1 - core, there)):
        chip = chip_of(slot >> 3, order, blk_index)
        k = 15 * (chip >> 1) + 7 * (chip & 1) + (slot & 7)
        pick = jnp.where(at == k, 1.0, 0.0).astype(jnp.bfloat16)
        for step, part in enumerate((part_0, part_1, part_2, part_3)):
            first = (blk_index // 4 - step & 3) * 4
            part = jnp.concatenate([part[c] for c in range(4)], 1)
            rows = jnp.dot(pick, part, preferred_element_type=jnp.float32).astype(jnp.bfloat16)
            for c in range(4):
                lo = 0
                for stage in STAGES:
                    each = 8 * stage
                    to = pl.multiple_of(GROUP * lo + (first + c) * each, 16)
                    out[pl.ds(to, each), :] = rows[lo : lo + each, 128 * c : 128 * c + 128]
                    lo += each


def slots_of_pieces(parts):
    shape = jax.ShapeDtypeStruct((GROUP * 128, 128), jnp.bfloat16)
    return pl.pallas_call(
        slots_kernel,
        out_shape=[shape, shape],
        in_specs=[VMEM] * 4,
        out_specs=[VMEM] * 2,
        compiler_params=ROOM,
        cost_estimate=SHORT,
        name="slots",
    )(*parts)


def products(pieces, rows_w, total):
    depth = rows_w.shape[0]
    most = 512 if total.shape[0] > 6 * PIECE else 768
    step = max(n for n in range(128, most + 1, 128) if depth % n == 0)
    total[...] = jnp.zeros_like(total)

    def body(n, carry):
        at = pl.ds(pl.multiple_of(n * step, 128), step)
        left = [piece[:, :, at].reshape(-1, step) for piece in pieces]
        total[...] += jnp.dot(
            jnp.concatenate(left, 0), rows_w[at, :], preferred_element_type=jnp.float32
        )
        return carry

    lax.fori_loop(0, depth // step, body, 0)


def ladder_kernel(first, pieces, rows_w, mine, other, total):
    core, blk_index = lax.axis_index("slab"), lax.axis_index("blk")
    products(pieces, rows_w, total)

    def body(n, carry):
        chip = chip_of(first + n, core, blk_index)
        value = total[pl.ds(pl.multiple_of(n * PIECE, PIECE), PIECE), :]

        @pl.when(chip // 8 == core)
        def _():
            mine[chip & 7] = value

        @pl.when(chip // 8 != core)
        def _():
            other[chip & 7] = value

        return carry

    lax.fori_loop(0, total.shape[0] // PIECE, body, 0)


def ladder_early_kernel(*refs):
    ladder_kernel(0, refs[:-4], *refs[-4:])


def ladder_late_kernel(*refs):
    ladder_kernel(STAGES[0], refs[:-6], refs[-6], *refs[-3:])


def ladder(stage, pieces, rows_w, before=()):
    out_columns = rows_w.shape[1]
    half = jax.ShapeDtypeStruct((8, PIECE, out_columns), jnp.float32)
    given = len(pieces) + 1
    return pl.pallas_call(
        ladder_late_kernel if stage else ladder_early_kernel,
        out_shape=[half, half],
        in_specs=[VMEM] * (given + len(before)),
        out_specs=[VMEM, VMEM],
        scratch_shapes=[pltpu.VMEM((STAGES[stage] * PIECE, out_columns), jnp.float32)],
        input_output_aliases={given + n: n for n in range(len(before))},
        compiler_params=ROOM,
        cost_estimate=SHORT,
        name="ladder_late" if stage else "ladder_early",
    )(*pieces, rows_w, *before)


def ladder_end_kernel(dims, mine, other, out, rows):
    out_columns = out.shape[1]
    column = lax.axis_index("blk") * out_columns
    column = column + lax.broadcasted_iota(jnp.int32, (1, out_columns), 1)
    block, c, d = column >> 12, column >> 6 & 63, column & 63
    size_first = jnp.where(block == 0, dims[0, 0], dims[1, 0])
    size_second = jnp.where(block == 0, dims[0, 1], dims[1, 1])
    keep = (c < size_first) & (d < size_second)

    def body(pair, carry):
        even = mine[2 * pair] + other[2 * pair]
        odd = mine[2 * pair + 1] + other[2 * pair + 1]
        both = jnp.concatenate([even[:56], even[56:] + odd[:8], odd[8:]], 0)
        rows[pl.ds(pl.multiple_of(pair * 120, 8), 120), :] = jnp.where(keep, both, 0.0)
        return carry

    lax.fori_loop(0, 4, body, 0)
    out[...] = rows[...].astype(jnp.bfloat16)


def ladder_end(block_dims, mine, other):
    shape = (480, mine.shape[2])
    return pl.pallas_call(
        ladder_end_kernel,
        out_shape=jax.ShapeDtypeStruct(shape, jnp.bfloat16),
        in_specs=[SMEM] + [VMEM] * 2,
        out_specs=VMEM,
        scratch_shapes=[pltpu.VMEM(shape, jnp.float32)],
        compiler_params=ROOM,
        cost_estimate=SHORT,
        name="ladder_end",
    )(block_dims, mine, other)


def turn(pieces, group_width, start, spread, turned):
    wide = GROUP * group_width
    count = sum(piece.shape[0] for piece in pieces)
    rows, each = count * PIECE, 8 * count
    n = 0
    for piece in pieces:

        def body(i, carry, piece=piece, n=n):
            part = piece[i, :, pl.ds(start, wide)].astype(jnp.float32)
            for b in range(wide // 128):
                at = pl.multiple_of((b * count + n + i) * PIECE, PIECE)
                spread[pl.ds(at, PIECE), :] = part[:, 128 * b : 128 * b + 128]
            return carry

        lax.fori_loop(0, piece.shape[0], body, 0)
        n += piece.shape[0]
    spread[wide // 128 * rows : wide // 128 * rows + rows, :] = jnp.zeros((rows, 128), jnp.float32)

    def columns(pair, carry):
        for c in range(GROUP):
            lo = c * group_width
            base = lo // 128
            blocks = [base] if lo % 128 + BS <= 128 else [base, base + 1]
            halves = []
            for odd in range(2):
                window = [
                    spread[pl.ds(b * rows + 2 * pair + odd, each, stride=8), :] for b in blocks
                ]
                window = jnp.concatenate(window, 1)
                halves.append(window[:, lo % 128 : lo % 128 + BS])
            at = pl.ds(pl.multiple_of(pair * 128, 128), 128)
            turned[c * each : (c + 1) * each, at] = jnp.concatenate(halves, 1).astype(turned.dtype)
        return carry

    lax.fori_loop(0, 4, columns, 0)


def first_part(core, plane):
    return (core == 0) == (plane < 3)


def group_starts(width, least, core, plane):
    first = jnp.where(core == 0, plane * (GROUP * width), 4 * GROUP * least)
    own = plane * (GROUP * least)
    return pl.multiple_of(first, 128), pl.multiple_of(own, 128)


def cycle_early_kernel(width, least, *refs):
    pieces, (first, own, spread) = refs[:-3], refs[-3:]
    core, plane = lax.axis_index("slab"), lax.axis_index("blk") & 3
    first_start, own_start = group_starts(width, least, core, plane)

    @pl.when(first_part(core, plane))
    def _():
        turn(pieces, width, first_start, spread, first)

    @pl.when(core == 1)
    def _():
        turn(pieces, least, own_start, spread, own)


def cycle_early(width, least, pieces):
    count = sum(p.shape[0] for p in pieces)
    shape = jax.ShapeDtypeStruct((GROUP * 8 * count, 8 * BS), jnp.bfloat16)
    blocks = GROUP * max(width, least) // 128 + 1
    return pl.pallas_call(
        functools.partial(cycle_early_kernel, width, least),
        out_shape=[shape, shape],
        in_specs=[VMEM] * len(pieces),
        out_specs=[VMEM, VMEM],
        scratch_shapes=[pltpu.VMEM((blocks * count * PIECE, 128), jnp.float32)],
        compiler_params=ROOM,
        cost_estimate=SHORT,
        name="cycle_early",
    )(*pieces)


def cycle_late_kernel(width, least, row, *refs):
    pieces, refs = refs[:-8], refs[-8:]
    before_first, before_own, slots_first, slots_own, first, own, spread, turned = refs
    core, plane = lax.axis_index("slab"), lax.axis_index("blk") & 3
    first_start, own_start = group_starts(width, least, core, plane)

    def add(slots, row, right):
        return lax.dot_general(
            slots[row : row + right.shape[0], :],
            right[...],
            (((0,), (0,)), ((), ())),
            preferred_element_type=jnp.float32,
        )

    def total(group_width, start, slots, before, out):
        turn(pieces, group_width, start, spread, turned)
        value = add(slots, 0, before) + add(slots, row, turned)
        for n in range(4):
            to = pl.multiple_of((plane ^ n) * 32, 32)
            out[pl.ds(to, 32), :] = value[32 * n : 32 * n + 32]

    first[...] = jnp.zeros_like(first)
    own[...] = jnp.zeros_like(own)

    @pl.when(first_part(core, plane))
    def _():
        total(width, first_start, slots_first, before_first, first)

    @pl.when(core == 1)
    def _():
        total(least, own_start, slots_own, before_own, own)

    @pl.when(core == 0)
    def _():
        own[...] = first[...]


def cycle_late(width, least, pieces, turned, slots_first, slots_own):
    count = STAGES[1]
    shape = jax.ShapeDtypeStruct((128, 8 * BS), jnp.float32)
    blocks = GROUP * max(width, least) // 128 + 1
    row = GROUP * 8 * STAGES[0]
    return pl.pallas_call(
        functools.partial(cycle_late_kernel, width, least, row),
        out_shape=[shape, shape],
        in_specs=[VMEM] * (4 + len(pieces)),
        out_specs=[VMEM, VMEM],
        scratch_shapes=[
            pltpu.VMEM((blocks * count * PIECE, 128), jnp.float32),
            pltpu.VMEM((GROUP * 8 * count, 8 * BS), jnp.bfloat16),
        ],
        compiler_params=ROOM,
        cost_estimate=SHORT,
        name="cycle_late",
    )(*pieces, *turned, slots_first, slots_own)


def together(*values):
    return lax.optimization_barrier(values)


def after(value, *others):
    return together(value, *others)[0]


def compacted(width, least, amplitudes, ladder_ints, cycle_ints, block_dims, moved):
    core = lax.axis_index("slab")
    blk_index = lax.axis_index("blk")
    plane, z = blk_index % 4, blk_index // 4
    wide_columns, narrow_columns = GROUP * width, GROUP * least
    columns = max(3 * wide_columns, wide_columns + 4 * narrow_columns)

    own = prep(width, least, columns, block_dims, amplitudes, moved)[None]
    near = [send(own, up(step)) for step in (1, 3)]
    plane_1 = send(own, first_axis)
    plane_2 = send(own, second_axis)
    plane_12 = send(plane_1, second_axis)
    ints, shares = together(ladder_ints, cycle_ints[0], own)[:2]
    moved_ints = ints.reshape(4, 4, 4 * BS, -1)[:, 3].reshape(GROUP * BS, -1)
    shares = [lax.dynamic_slice_in_dim(shares, (z + step) % 4 * 128, 128, 2) for step in range(4)]
    rows_w = own_rows(ints, width, least, columns, core)
    far = send(after(own, *near), up(2))
    dims = after(block_dims, own)
    allowed = cycle_allowed(dims, core, blk_index, 32, 8 * BS).astype(jnp.float32)
    near, moved_ints, rows_w, allowed, *shares = together(
        jnp.concatenate(near), moved_ints, rows_w, allowed, *shares, plane_1, plane_2, plane_12
    )[:8]
    near_1 = send(near, first_axis)
    near_2 = send(near, second_axis)
    moved_ints = to_other_core(moved_ints, (0,))
    *shares, rows_w, moved_ints, near_2, near_1, far = together(
        *shares, rows_w, moved_ints, near_2, near_1, far
    )
    cut = 4 * narrow_columns
    moved_rows = pad_rows(cut_rows(moved_ints, width), columns - cut)
    rows_w = lax.dynamic_update_slice(
        rows_w, jnp.where(core == 0, rows_w[cut:], moved_rows), (cut, 0)
    )
    far_1 = send(far, first_axis)
    far_2 = send(far, second_axis)
    near_12 = send(near_1, second_axis)
    shares[3] = send(shares[3], up(3))
    shares[2] = send(shares[2], up(2))
    shares[1] = send(after(shares[1], shares[3]), up(1))
    early = [own, plane_1, plane_2, plane_12, near, near_1, near_2]
    sums = ladder(0, early, rows_w)
    turned = cycle_early(width, least, early)
    far_1, far_2, near_12, sums, turned, *shares = together(
        far_1, far_2, near_12, sums, turned, *shares
    )
    far_12 = send(far_1, second_axis)
    slots, there = slots_of_pieces(shares)
    there = [
        lax.ppermute(part, AXES, [(2 * chip, 2 * chip + 1) for chip in LAST_CHIPS])
        for part in jnp.split(there, 2)
    ]
    near_12, slots, far_12, *there = together(near_12, slots, far_12, *there)
    slots_first = jnp.where(core == 0, slots, jnp.concatenate(there))
    late = [near_12, far, far_1, far_2, far_12]
    terms = cycle_late(width, least, late, turned, slots_first, slots)
    pairs = [(2 * chip + 1, 2 * chip) for chip in LAST_CHIPS]
    last_group = lax.ppermute(terms[0], AXES, pairs)
    mine, other = ladder(1, late, rows_w, after(sums, terms[1]))
    other = to_other_core(other, (0, 1))
    term = (terms[1] + last_group).reshape(4, 32, 8 * BS)
    parts = [send(term[n], target) for n, target in ((1, along_x), (2, along_y), (3, across))]
    ladder_res = ladder_end(block_dims, mine, other)
    parts = together(term[0], *parts, ladder_res)[:4]
    cycle_sum = parts[0] + parts[1] + parts[2] + parts[3]
    cycle_res = (cycle_sum * allowed).astype(jnp.bfloat16)[None]
    return (ladder_res, cycle_res)


WIDTHS = (48, 56, 64)


def local(amplitudes, ladder_ints, cycle_ints, block_dims):
    moved = to_other_core(amplitudes, (0,))
    fits = [block_dims[0, 1] > width for width in WIDTHS[:-1]]
    choice = sum(fit.astype(jnp.int32) for fit in fits)
    choice = jnp.where(block_dims[1, 1] <= LEAST, choice, len(WIDTHS))
    branches = [functools.partial(compacted, width, LEAST) for width in WIDTHS]
    branches.append(functools.partial(compacted, BS, BS))
    return lax.switch(
        choice, branches, amplitudes, ladder_ints, cycle_ints, block_dims, moved
    )


def solution(mesh):
    in_specs = (P("blk", "slab"), P("slab", "blk"), P("slab", "blk", None, None), P())
    out_specs = (P("slab", "blk"), P("slab", "blk", None))
    body = local if dict(mesh.shape) == {"blk": 16, "slab": 2} else plain
    return jax.shard_map(body, mesh=mesh, in_specs=in_specs, out_specs=out_specs, check_vma=False)
```
